32 devices in a mesh: frame: 16 (over z, x, core), mod: 2 (over y).
Axes of the slice: x: 2, y: 2, z: 4, core: 2. Of those that a mesh axis runs over, the one named last changes fastest.
Arguments:
- frames: bfloat16 [2048, 8192], P('frame', 'mod'), may hold values from 0.2 to 64, as said below
- cycle_label: int32 [8192], P('mod'), may hold values from 0 to 15, as said below
- good_pixel: int32 [8192], P('mod'), may hold values from 0 to 1
Outputs:
- correlation: float32 [16, 2048, 1024], P('mod', 'frame')
The draws below stay inside these ranges and needn't reach their ends.
Inputs may be any that keep to these rules, and one draw needn't show every extreme that they name: `cycle_label`: on every block of 4096 consecutive pixels each of the 16 cycles holds exactly 256 pixels, at least one of them with good_pixel 1. `frames`: positive intensities.
All inputs are finite; a program needn't handle non-finite values.
Results may differ from the reference program's by a relative error of at most 0.0003.
Values may be sent and summed in bfloat16 or wider, within the bound.
No kernel may reach another device: no remote copies, remote signals or barrier semaphores. Data moves between devices by JAX's collectives and lax.ppermute only.
A program may use at most 64 MiB of HBM per device.

```python
import math
import jax
import jax.numpy as jnp
from jax import lax

CYCLES = 16
LAG = 1024
FB = 128
PIX_DEV = 4096
FRAMES = 2048
PIXELS = 8192


def pixel_layout(key):
    base_key = jax.random.fold_in(key, 11)
    key_order, key_good = jax.random.split(base_key, 2)
    groups = PIXELS // PIX_DEV
    order_keys = jax.random.split(key_order, groups)
    rank_order = jax.vmap(lambda one_key: jax.random.permutation(one_key, PIX_DEV))(order_keys)
    random_good = (jax.random.randint(key_good, (groups, PIX_DEV), 0, 8, dtype=jnp.int32) > 0).astype(jnp.int32)
    forced = rank_order < CYCLES
    labels = (rank_order % CYCLES).reshape(PIXELS).astype(jnp.int32)
    good_flag = jnp.where(forced, 1, random_good).reshape(PIXELS).astype(jnp.int32)
    return (labels, good_flag)


def draw_cycle_label(key, part):
    return pixel_layout(key)[0]


def draw_good_pixel(key, part):
    return pixel_layout(key)[1]


def draw_frames(key, part):
    key_level, key_pixel, key_speckle = jax.random.split(jax.random.fold_in(key, 5), 3)
    frame_level = jax.random.uniform(key_level, (FRAMES, 1), jnp.float32, 0.0, math.log(4.0))
    pixel_gain = jax.random.uniform(key_pixel, (1, PIXELS), jnp.float32, 0.0, math.log(4.0))
    speckle = jnp.exp(jax.random.uniform(key_speckle, (FRAMES, PIXELS), jnp.float32, math.log(0.25), math.log(4.0)))
    return (jnp.exp(frame_level) * jnp.exp(pixel_gain) * speckle).astype(jnp.bfloat16)


def setup_inputs(seed: int = 0) -> dict:
    key_list = jax.random.split(jax.random.key(seed), 4)
    frames = draw_frames(jax.random.fold_in(key_list[3], 71), 0)
    cycle_label = draw_cycle_label(jax.random.fold_in(key_list[3], 71), 0)
    good_pixel = draw_good_pixel(jax.random.fold_in(key_list[3], 71), 0)
    return dict(frames=frames, cycle_label=cycle_label, good_pixel=good_pixel)


def reference(frames, cycle_label, good_pixel):
    cycle_ids = jnp.arange(CYCLES, dtype=jnp.int32)
    weights = jnp.where(cycle_label[:, None] == cycle_ids[None, :], good_pixel[:, None], 0).astype(jnp.bfloat16)
    cycle_counts = jnp.sum(weights.astype(jnp.float32), axis=0)
    cycle_sums = jnp.dot(frames, weights, preferred_element_type=jnp.float32)
    intensity = frames.astype(jnp.float32)
    weight_rows = weights.astype(jnp.float32).T
    padded = jnp.concatenate([intensity, jnp.zeros((LAG, intensity.shape[1]), jnp.float32)], axis=0)
    padded_sums = jnp.concatenate([cycle_sums, jnp.zeros((LAG, CYCLES), jnp.float32)], axis=0)
    window_width = FB + LAG

    def one_block(block_index):
        first_row = (block_index * FB).astype(jnp.int32)
        block_rows = lax.dynamic_slice_in_dim(intensity, first_row, FB, 0)
        window = lax.dynamic_slice_in_dim(padded, first_row, window_width, 0)
        weighted = block_rows[None, :, :] * weight_rows[:, None, :]
        gram_tile = jnp.einsum("rfp,gp->rfg", weighted, window, precision=lax.Precision.HIGHEST)
        later_sums = lax.dynamic_slice_in_dim(padded_sums, first_row, window_width, 0).T
        earlier = later_sums[:, :FB]
        frame_at = first_row + jnp.arange(window_width, dtype=jnp.int32)
        in_range = frame_at < FRAMES
        safe_sums = jnp.where(in_range[None, :], later_sums, 1.0)
        normalized = gram_tile * cycle_counts[:, None, None] / (earlier[:, :, None] * safe_sums[:, None, :])
        normalized = jnp.where(in_range[None, None, :], normalized, 0.0)
        flattened = jnp.pad(normalized.reshape(CYCLES, FB * window_width), ((0, 0), (0, FB)))
        return flattened.reshape(CYCLES, FB, window_width + 1)[:, :, :LAG]

    blocks = lax.map(one_block, jnp.arange(FRAMES // FB, dtype=jnp.int32))
    return blocks.transpose(1, 0, 2, 3).reshape(CYCLES, FRAMES, LAG)
```

```python
import functools

import jax
import jax.numpy as jnp
from jax import lax
from jax.experimental import pallas as pl
from jax.experimental.pallas import tpu as pltpu
from jax.sharding import PartitionSpec as P

CYCLES = 16
LAG = 1024
LANES = 128
SUBLANES = 8
CHUNK = 256
VMEM_LIMIT = 48 * 1024 * 1024


def order_kernel(groups_ref, frames_ref, label_ref, good_ref, *rest, group_cycles):
    group_refs, (counts_ref, key_ref) = rest[:-2], rest[-2:]
    chunks = label_ref.shape[0]
    rows = chunks * CYCLES
    per_cycle = frames_ref.shape[1] // CYCLES
    cycle_iota = lax.broadcasted_iota(jnp.int32, (CYCLES, CHUNK), 0)
    member = jnp.concatenate(
        [
            jnp.where(label_ref[chunk : chunk + 1, :] == cycle_iota, 1.0, 0.0)
            for chunk in range(chunks)
        ],
        axis=0,
    )
    good = jnp.concatenate(
        [
            jnp.broadcast_to(good_ref[chunk : chunk + 1, :], (CYCLES, CHUNK))
            for chunk in range(chunks)
        ],
        axis=0,
    )
    member_b = member.astype(jnp.bfloat16)
    up = lax.broadcasted_iota(jnp.int32, (rows, rows), 0)
    across = lax.broadcasted_iota(jnp.int32, (rows, rows), 1)
    same = lax.rem(up, CYCLES) == lax.rem(across, CYCLES)
    chunk_before = jnp.where(same & (across < up), 1.0, 0.0).astype(jnp.bfloat16)
    before = (
        lax.broadcasted_iota(jnp.int32, (CHUNK, CHUNK), 0)
        < lax.broadcasted_iota(jnp.int32, (CHUNK, CHUNK), 1)
    )
    before = jnp.where(before, 1.0, 0.0).astype(jnp.bfloat16)
    ones = jnp.ones((CHUNK, CHUNK), jnp.bfloat16)
    dot = functools.partial(jnp.dot, preferred_element_type=jnp.float32)
    earlier = dot(chunk_before, member_b).astype(jnp.bfloat16)
    rank = dot(member_b, before) + dot(earlier, ones)
    used = (member > 0.0) & (good > 0)
    key_ref[...] = jnp.where(used, rank, -1.0)

    of_cycle = jnp.where(
        lax.broadcasted_iota(jnp.int32, (CYCLES, rows), 0)
        == lax.rem(lax.broadcasted_iota(jnp.int32, (CYCLES, rows), 1), CYCLES),
        1.0,
        0.0,
    ).astype(jnp.bfloat16)
    per_lane = dot(of_cycle, jnp.where(used, 1.0, 0.0).astype(jnp.bfloat16))
    counts_ref[...] = dot(per_lane.astype(jnp.bfloat16), jnp.ones((CHUNK, LANES), jnp.bfloat16))

    slots = [
        (lax.broadcasted_iota(jnp.int32, (16, CHUNK), 0) + first).astype(jnp.float32).astype(jnp.bfloat16)
        for first in range(0, per_cycle, 16)
    ]
    one = jnp.ones((16, CHUNK), jnp.bfloat16)
    zero = jnp.zeros((16, CHUNK), jnp.bfloat16)
    frames = frames_ref[...]
    for number, group_ref in enumerate(group_refs):
        first_cycle = groups_ref[number] * group_cycles

        @pl.loop(0, group_cycles)
        def _(cycle):
            tiles = []
            for chunk in range(chunks):
                key = key_ref[pl.ds(chunk * CYCLES + first_cycle + cycle, 1), :]
                key = jnp.broadcast_to(key, (16, CHUNK)).astype(jnp.bfloat16)
                tiles.append(
                    jnp.concatenate([jnp.where(key == slot, one, zero) for slot in slots], axis=0)
                )
            chosen = jnp.concatenate(tiles, axis=1)
            picked = lax.dot_general(
                chosen, frames, (((1,), (1,)), ((), ())), preferred_element_type=jnp.float32
            )
            start = pl.multiple_of(cycle * per_cycle, per_cycle)
            group_ref[pl.ds(start, per_cycle), :] = picked.astype(jnp.bfloat16)


def order_pixels(groups, frames, label, good, group_cycles):
    block_rows, pix_count = frames.shape
    pixels = group_cycles * (pix_count // CYCLES)
    rows = pix_count // CHUNK * CYCLES
    vmem = pl.BlockSpec(memory_space=pltpu.VMEM)
    out_shape = [
        jax.ShapeDtypeStruct((pixels, block_rows), jnp.bfloat16) for _ in range(groups.shape[0])
    ] + [jax.ShapeDtypeStruct((CYCLES, LANES), jnp.float32)]
    return pl.pallas_call(
        functools.partial(order_kernel, group_cycles=group_cycles),
        out_shape=out_shape,
        in_specs=[pl.BlockSpec(memory_space=pltpu.SMEM), vmem, vmem, vmem],
        out_specs=[vmem] * len(out_shape),
        scratch_shapes=[pltpu.VMEM((rows, CHUNK), jnp.float32)],
        compiler_params=pltpu.CompilerParams(vmem_limit_bytes=VMEM_LIMIT),
        cost_estimate=pl.CostEstimate(
            flops=2 * pixels * groups.shape[0] * pix_count * block_rows,
            bytes_accessed=2 * pix_count * block_rows,
            transcendentals=0,
        ),
    )(groups, frames, label.reshape(-1, CHUNK), good.reshape(-1, CHUNK))


def gram_kernel(place_ref, counts_ref, *rest, pieces, frame_count, first_cycle_step):
    window_refs, (mine_ref, theirs_ref, window, gram, later, earlier) = rest[:-6], rest[-6:]
    core, chip, first_cycle = place_ref[0], place_ref[1], place_ref[2]
    block = mine_ref.shape[1]
    pieces_count = len(pieces)
    pair_count = len(window_refs) // pieces_count
    for pair in range(pair_count):
        for relative in range(2):
            at = pl.multiple_of((2 * pair) * block + (relative ^ core) * block, block)
            row = 0
            for piece in range(pieces_count):
                ref = window_refs[pair * pieces_count + piece]
                for source in range(ref.shape[1]):
                    height = ref.shape[2]
                    window[row : row + height, pl.ds(at, block)] = ref[relative, source]
                    row += height
    whole = window[...]
    own = window[:, : 2 * block]
    gram[...] = lax.dot_general(
        own, whole, (((0,), (0,)), ((), ())), preferred_element_type=jnp.float32
    )
    depth, width = whole.shape
    sums = lax.dot_general(
        jnp.ones((SUBLANES, depth), jnp.bfloat16),
        whole,
        (((1,), (0,)), ((), ())),
        preferred_element_type=jnp.float32,
    )
    frame_at = chip * (2 * block) + lax.broadcasted_iota(jnp.int32, (SUBLANES, width), 1)
    later[...] = jnp.where(frame_at < frame_count, 1.0 / sums, 0.0)
    cycle = first_cycle + pl.program_id(0)
    count = counts_ref[pl.ds(cycle, 1), :]
    own_sums = lax.dot_general(
        own,
        jnp.ones((depth, LANES), jnp.bfloat16),
        (((0,), (0,)), ((), ())),
        preferred_element_type=jnp.float32,
    )
    earlier[...] = count / own_sums
    lane = lax.broadcasted_iota(jnp.int32, (SUBLANES, LANES), 1)
    sublane = lax.broadcasted_iota(jnp.int32, (SUBLANES, LANES), 0)
    tiles = LAG // LANES
    for out_ref, position in ((mine_ref, core), (theirs_ref, 1 - core)):
        base = pl.multiple_of(position * block, block)
        for first in range(0, block, SUBLANES):
            factor = earlier[pl.ds(base + first, SUBLANES), :]
            skip = first % LANES
            kept = lane + sublane < LANES - skip
            turned = lax.rem(lane + sublane + skip, LANES)
            rolled = []
            for tile in range(tiles + 1):
                column = pl.multiple_of(base + (first // LANES + tile) * LANES, LANES)
                value = gram[pl.ds(base + first, SUBLANES), pl.ds(column, LANES)]
                value = value * factor * later[:, pl.ds(column, LANES)]
                rolled.append(
                    jnp.take_along_axis(value, turned, axis=1, mode="promise_in_bounds")
                )
            for tile in range(tiles):
                out_ref[0, first : first + SUBLANES, tile * LANES : (tile + 1) * LANES] = jnp.where(
                    kept, rolled[tile], rolled[tile + 1]
                )


def grams(place, counts, windows, frame_count, group_cycles, out_cycles):
    flat = [piece for pair in windows for piece in pair]
    pieces = [piece.shape[1] for piece in windows[0]]
    block = flat[0].shape[-1]
    per_cycle = flat[0].shape[2] // group_cycles
    depth = sum(pieces) * per_cycle
    width = 2 * len(windows) * block
    kernel = functools.partial(
        gram_kernel, pieces=pieces, frame_count=frame_count, first_cycle_step=group_cycles
    )
    in_specs = [pl.BlockSpec((CYCLES, LANES), lambda i, place: (0, 0))]
    in_specs += [
        pl.BlockSpec((2, piece.shape[1], per_cycle, block), lambda i, place: (0, 0, i, 0))
        for piece in flat
    ]
    grid_spec = pltpu.PrefetchScalarGridSpec(
        num_scalar_prefetch=1,
        grid=(group_cycles,),
        in_specs=in_specs,
        out_specs=[
            pl.BlockSpec((1, block, LAG), lambda i, place: (place[0] * group_cycles + i, 0, 0)),
            pl.BlockSpec((1, block, LAG), lambda i, place: (i, 0, 0)),
        ],
        scratch_shapes=[
            pltpu.VMEM((depth, width), jnp.bfloat16),
            pltpu.VMEM((2 * block, width), jnp.float32),
            pltpu.VMEM((SUBLANES, width), jnp.float32),
            pltpu.VMEM((2 * block, LANES), jnp.float32),
        ],
    )
    return pl.pallas_call(
        kernel,
        grid_spec=grid_spec,
        out_shape=[
            jax.ShapeDtypeStruct((out_cycles, block, LAG), jnp.float32),
            jax.ShapeDtypeStruct((group_cycles, block, LAG), jnp.float32),
        ],
        compiler_params=pltpu.CompilerParams(vmem_limit_bytes=VMEM_LIMIT),
        cost_estimate=pl.CostEstimate(
            flops=2 * group_cycles * depth * width * 2 * block,
            bytes_accessed=2 * group_cycles * (depth * width + 4 * block * LAG),
            transcendentals=0,
        ),
    )(place, counts, *flat)


def fill_kernel(place_ref, whole_ref, part_ref, out_ref):
    out_ref[...] = part_ref[...]


def fill(place, whole, part):
    count, block, lags = part.shape
    grid_spec = pltpu.PrefetchScalarGridSpec(
        num_scalar_prefetch=1,
        grid=(count,),
        in_specs=[
            pl.BlockSpec(memory_space=pl.ANY),
            pl.BlockSpec((1, block, lags), lambda i, place: (i, 0, 0)),
        ],
        out_specs=pl.BlockSpec(
            (1, block, lags), lambda i, place: ((1 - place[0]) * count + i, 0, 0)
        ),
    )
    return pl.pallas_call(
        fill_kernel,
        grid_spec=grid_spec,
        out_shape=jax.ShapeDtypeStruct(whole.shape, whole.dtype),
        input_output_aliases={1: 0},
        cost_estimate=pl.CostEstimate(flops=0, bytes_accessed=8 * part.size, transcendentals=0),
    )(place, whole, part)


def shifted(value, pairs_down):
    step = 2 * pairs_down
    count = lax.axis_size("frame")
    return lax.ppermute(value, "frame", [(source, source - step) for source in range(step, count)])


def other_pair(value):
    count = lax.axis_size("frame")
    return lax.ppermute(value, "frame", [(source, source ^ 2) for source in range(count)])


def other_core(value):
    count = lax.axis_size("frame")
    return lax.ppermute(value, "frame", [(source, source ^ 1) for source in range(count)])


def to_mod(value, step, core_flip):
    frames, mods = lax.axis_size("frame"), lax.axis_size("mod")
    pairs = [
        (frame * mods + mod, (frame ^ core_flip) * mods + (mod + step) % mods)
        for frame in range(frames)
        for mod in range(mods)
    ]
    return lax.ppermute(value, ("frame", "mod"), pairs)


def shards(frames, cycle_label, good_pixel):
    mods = lax.axis_size("mod")
    cycle_dev = CYCLES // mods
    group_cycles = cycle_dev // 2
    mod, frame = lax.axis_index("mod"), lax.axis_index("frame")
    core, chip = frame % 2, frame // 2
    block = frames.shape[0]
    assert LAG == 8 * block and block == LANES

    def ordered(step):
        target = (mod + step) % mods
        groups = jnp.stack([target * 2 + core, target * 2 + 1 - core]).astype(jnp.int32)
        return order_pixels(groups, frames, cycle_label, good_pixel, group_cycles)

    kept, sent, counts = ordered(0)
    counts = lax.psum(counts, "mod")
    first = jnp.stack([kept, other_core(sent)])[:, None]
    rest = []
    for step in range(1, mods):
        same, flipped, _ = ordered(step)
        rest.append(jnp.stack([to_mod(same, step, 0), to_mod(flipped, step, 1)]))
    pieces = [first, jnp.stack(rest, axis=1)]
    later_chip = chip % 2 == 1
    windows = [[] for _ in range(5)]
    for own in pieces:
        two = shifted(own, 2)
        four = shifted(two, 2)
        one = other_pair(jnp.where(later_chip, own, two))
        three = other_pair(jnp.where(later_chip, two, four))
        for window, value in zip(windows, (own, one, two, three, four)):
            window.append(value)
    place = jnp.stack([core, chip, mod * cycle_dev + core * group_cycles]).astype(jnp.int32)
    frame_count = block * lax.axis_size("frame")
    whole, theirs = grams(place, counts, windows, frame_count, group_cycles, cycle_dev)
    return fill(place, whole, other_core(theirs))


def solution(mesh):
    placed = (P("frame", "mod"), P("mod"), P("mod"))
    return jax.shard_map(
        shards, mesh=mesh, in_specs=placed, out_specs=P("mod", "frame", None), check_vma=False
    )
```

```python
import functools

import jax
import jax.numpy as jnp
from jax import lax
from jax.experimental import pallas as pl
from jax.experimental.pallas import tpu as pltpu
from jax.sharding import PartitionSpec as P

CYCLES = 16
LAG = 1024
LANES = 128
SUBLANES = 8
PACKED = 16
CHUNK = 256
VMEM_LIMIT = 40 * 1024 * 1024

SMEM_SPEC = pl.BlockSpec(memory_space=pltpu.SMEM)
VMEM_SPEC = pl.BlockSpec(memory_space=pltpu.VMEM)
ANY_SPEC = pl.BlockSpec(memory_space=pl.ANY)

dot = functools.partial(jnp.dot, preferred_element_type=jnp.float32)


def params():
    return pltpu.CompilerParams(vmem_limit_bytes=VMEM_LIMIT)


def estimate(flops, moved):
    return pl.CostEstimate(flops=flops, bytes_accessed=moved, transcendentals=0)


def ones_where(condition):
    return jnp.where(condition, 1.0, 0.0).astype(jnp.bfloat16)


def iota(shape, dimension):
    return lax.broadcasted_iota(jnp.int32, shape, dimension)


def rank_kernel(label_ref, good_ref, key_ref, counts_ref):
    chunks = label_ref.shape[0] // CHUNK
    rows = chunks * CYCLES
    cycle_at = iota((CYCLES, CHUNK), 0)
    labels = [label_ref[pl.ds(at * CHUNK, CHUNK)].reshape(1, CHUNK) for at in range(chunks)]
    goods = [good_ref[pl.ds(at * CHUNK, CHUNK)].reshape(1, CHUNK) for at in range(chunks)]
    member = jnp.concatenate([jnp.where(one == cycle_at, 1.0, 0.0) for one in labels], axis=0)
    good = jnp.concatenate([jnp.broadcast_to(one, (CYCLES, CHUNK)) for one in goods], axis=0)
    member_b = member.astype(jnp.bfloat16)
    up, across = iota((rows, rows), 0), iota((rows, rows), 1)
    same = lax.rem(up, CYCLES) == lax.rem(across, CYCLES)
    chunk_before = ones_where(same & (across < up))
    before = ones_where(iota((CHUNK, CHUNK), 0) < iota((CHUNK, CHUNK), 1))
    earlier = dot(chunk_before, member_b).astype(jnp.bfloat16)
    rank = dot(member_b, before) + dot(earlier, jnp.ones((CHUNK, CHUNK), jnp.bfloat16))
    used = (member > 0.0) & (good > 0)
    key_ref[...] = jnp.where(used, rank, -1.0)
    of_cycle = ones_where(iota((CYCLES, rows), 0) == lax.rem(iota((CYCLES, rows), 1), CYCLES))
    per_lane = dot(of_cycle, ones_where(used))
    counts_ref[...] = dot(per_lane.astype(jnp.bfloat16), jnp.ones((CHUNK, LANES), jnp.bfloat16))


def rank_pixels(label, good):
    rows = label.shape[0] // CHUNK * CYCLES
    return pl.pallas_call(
        rank_kernel,
        out_shape=[
            jax.ShapeDtypeStruct((rows, CHUNK), jnp.float32),
            jax.ShapeDtypeStruct((CYCLES, LANES), jnp.float32),
        ],
        in_specs=[VMEM_SPEC, VMEM_SPEC],
        out_specs=[VMEM_SPEC, VMEM_SPEC],
        compiler_params=params(),
        cost_estimate=estimate(6 * rows * CHUNK * CHUNK, 8 * label.shape[0]),
    )(label, good)


def order_kernel(place_ref, key_ref, own_ref, other_ref, *rest, step, mods, parts):
    part_refs, frames_ref = rest[:-1], rest[-1]
    block = own_ref.shape[0]
    chunks = key_ref.shape[0] // CYCLES
    per_cycle = own_ref.shape[1] // CYCLES
    core, mod = place_ref[0], place_ref[2]
    group_cycles = sum(parts)
    first_cycle = (lax.rem(mod + step, mods) * 2 + core) * group_cycles
    frames_ref[pl.ds(pl.multiple_of(core * block, block), block), :] = own_ref[...]
    frames_ref[pl.ds(pl.multiple_of((1 - core) * block, block), block), :] = other_ref[...]
    frames = frames_ref[...]
    slots = [
        (iota((PACKED, CHUNK), 0) + first).astype(jnp.float32).astype(jnp.bfloat16)
        for first in range(0, per_cycle, PACKED)
    ]
    one = jnp.ones((PACKED, CHUNK), jnp.bfloat16)
    zero = jnp.zeros((PACKED, CHUNK), jnp.bfloat16)
    done = 0
    for part_ref, part in zip(part_refs, parts):
        for cycle in range(part):
            tiles = []
            for chunk in range(chunks):
                key = key_ref[pl.ds(chunk * CYCLES + first_cycle + done + cycle, 1), :]
                key = jnp.broadcast_to(key, (PACKED, CHUNK)).astype(jnp.bfloat16)
                tiles.append(
                    jnp.concatenate([jnp.where(key == slot, one, zero) for slot in slots], axis=0)
                )
            picked = lax.dot_general(
                jnp.concatenate(tiles, axis=1),
                frames,
                (((1,), (1,)), ((), ())),
                preferred_element_type=jnp.float32,
            )
            part_ref[cycle * per_cycle : (cycle + 1) * per_cycle, :] = picked.astype(jnp.bfloat16)
        done += part


def order_pixels(place, key, own, other, step, mods, parts):
    block, pix_count = own.shape
    per_cycle = pix_count // CYCLES
    return pl.pallas_call(
        functools.partial(order_kernel, step=step, mods=mods, parts=parts),
        out_shape=[
            jax.ShapeDtypeStruct((part * per_cycle, 2 * block), jnp.bfloat16) for part in parts
        ],
        in_specs=[SMEM_SPEC] + [VMEM_SPEC] * 3,
        out_specs=[VMEM_SPEC] * len(parts),
        scratch_shapes=[pltpu.VMEM((2 * block, pix_count), jnp.bfloat16)],
        compiler_params=params(),
        cost_estimate=estimate(
            4 * sum(parts) * per_cycle * pix_count * block, 4 * pix_count * block
        ),
    )(place, key, own, other)


def gram_kernel(place_ref, counts_ref, *rest, pieces, pairs, choice, frame_count, cycle_step, offset, phase, chained):
    inputs = rest[: (1 + pairs) * pieces]
    mine_ref, theirs_ref, gram, later, earlier = rest[-5:]
    core, chip, mod = place_ref[0], place_ref[1], place_ref[2]
    block = mine_ref.shape[1]
    lags = mine_ref.shape[2]

    def piece_rows(number):
        refs = inputs[number * pieces : (number + 1) * pieces]
        return jnp.concatenate([ref[at] for ref in refs for at in range(ref.shape[0])], axis=0)

    own = piece_rows(0)
    columns = [piece_rows(1 + number) for number in range(pairs)]
    at, even, odd = choice
    chosen = jnp.where(lax.rem(chip, 2) == 0, columns[even], columns[odd])
    columns = [value for number, value in enumerate(columns) if number not in (even, odd)]
    columns.insert(at, chosen)
    if phase == 0:
        columns.insert(0, own)
    whole = jnp.concatenate(columns, axis=1)
    depth, width = whole.shape
    own_rows = own.T
    gram[...] = dot(own_rows, whole)
    sums = dot(jnp.ones((PACKED, depth), jnp.bfloat16), whole)[:SUBLANES]
    frame_at = chip * (2 * block) + phase * lags + iota((SUBLANES, width), 1)
    later[...] = jnp.where(frame_at < frame_count, 1.0 / sums, 0.0)
    cycle = (mod * 2 + core) * cycle_step + offset + pl.program_id(0)
    count = counts_ref[pl.ds(cycle, 1), :]
    earlier[...] = count / dot(own_rows, jnp.ones((depth, LANES), jnp.bfloat16))
    lane, sublane = iota((SUBLANES, LANES), 1), iota((SUBLANES, LANES), 0)
    tiles = lags // LANES
    for out_ref, position in ((mine_ref, core), (theirs_ref, 1 - core)):
        base = pl.multiple_of(position * block, block)
        for first in range(0, block, SUBLANES):
            factor = earlier[pl.ds(base + first, SUBLANES), :]
            kept = lane + sublane < LANES - first
            turned = lax.rem(lane + sublane + first, LANES)
            rolled = []
            for tile in range(tiles + 1):
                column = pl.multiple_of(base + tile * LANES, LANES)
                value = gram[pl.ds(base + first, SUBLANES), pl.ds(column, LANES)]
                value = value * factor * later[:, pl.ds(column, LANES)]
                rolled.append(jnp.take_along_axis(value, turned, axis=1, mode="promise_in_bounds"))
            for tile in range(tiles):
                out_ref[0, first : first + SUBLANES, tile * LANES : (tile + 1) * LANES] = jnp.where(
                    kept, rolled[tile], rolled[tile + 1]
                )


def grams(place, counts, whole, windows, choice, sizes, phase, frame_count):
    group_cycles, cycle_dev, offset, count, per_cycle = sizes
    flat = [piece for pair in windows for piece in pair]
    pieces = len(windows[0])
    chip_block = flat[0][0].shape[-1]
    block = chip_block // 2
    depth = sum(piece.shape[0] for piece, _ in windows[0]) * per_cycle
    lags = LAG // 2
    width = lags + chip_block
    kernel = functools.partial(
        gram_kernel,
        pieces=pieces,
        pairs=len(windows) - 1,
        choice=choice,
        frame_count=frame_count,
        cycle_step=group_cycles,
        offset=offset,
        phase=phase,
        chained=whole is not None,
    )

    def piece_spec(piece, first):
        return pl.BlockSpec(
            (piece.shape[0], per_cycle, chip_block), lambda i, place: (0, first + i, 0)
        )

    in_specs = [pl.BlockSpec((CYCLES, LANES), lambda i, place: (0, 0))]
    in_specs += [piece_spec(piece, first) for piece, first in flat]
    operands = [place, counts] + [piece for piece, _ in flat]
    aliases = {}
    if whole is not None:
        aliases = {len(operands): 0}
        operands.append(whole)
        in_specs.append(ANY_SPEC)
    grid_spec = pltpu.PrefetchScalarGridSpec(
        num_scalar_prefetch=1,
        grid=(count,),
        in_specs=in_specs,
        out_specs=[
            pl.BlockSpec(
                (1, block, lags), lambda i, place: (place[0] * group_cycles + offset + i, 0, phase)
            ),
            pl.BlockSpec((1, block, lags), lambda i, place: (i, 0, 0)),
        ],
        scratch_shapes=[
            pltpu.VMEM((chip_block, width), jnp.float32),
            pltpu.VMEM((SUBLANES, width), jnp.float32),
            pltpu.VMEM((chip_block, LANES), jnp.float32),
        ],
    )
    return pl.pallas_call(
        kernel,
        grid_spec=grid_spec,
        out_shape=[
            jax.ShapeDtypeStruct((cycle_dev, block, LAG), jnp.float32),
            jax.ShapeDtypeStruct((count, block, lags), jnp.float32),
        ],
        input_output_aliases=aliases,
        compiler_params=params(),
        cost_estimate=estimate(
            2 * count * depth * width * chip_block, 8 * count * chip_block * lags
        ),
    )(*operands)


def fill_kernel(place_ref, *rest, spots):
    count = len(spots)
    part_refs, out_ref, sems = rest[:count], rest[-2], rest[-1]
    copies = []
    for number, (part_ref, (group, offset, lag)) in enumerate(zip(part_refs, spots)):
        cycles, _, lags = part_ref.shape
        first = (1 - place_ref[0]) * group + offset
        copies.append(
            pltpu.make_async_copy(
                part_ref,
                out_ref.at[pl.ds(first, cycles), :, pl.ds(lag, lags)],
                sems.at[number],
            )
        )
    for copy in copies:
        copy.start()
    for copy in copies:
        copy.wait()


def fill(place, whole, parts, spots):
    return pl.pallas_call(
        functools.partial(fill_kernel, spots=spots),
        out_shape=jax.ShapeDtypeStruct(whole.shape, whole.dtype),
        in_specs=[SMEM_SPEC] + [ANY_SPEC] * (len(parts) + 1),
        out_specs=ANY_SPEC,
        scratch_shapes=[pltpu.SemaphoreType.DMA((len(parts),))],
        input_output_aliases={1 + len(parts): 0},
        compiler_params=params(),
        cost_estimate=estimate(0, 8 * sum(part.size for part in parts)),
    )(place, *parts, whole)


def shifted(value, pairs_down):
    step = 2 * pairs_down
    count = lax.axis_size("frame")
    return lax.ppermute(value, "frame", [(source, source - step) for source in range(step, count)])


def other_pair(value, parity=None):
    count = lax.axis_size("frame")
    sources = [at for at in range(count) if parity is None or at // 2 % 2 == parity]
    return lax.ppermute(value, "frame", [(source, source ^ 2) for source in sources])


def other_core(value):
    count = lax.axis_size("frame")
    return lax.ppermute(value, "frame", [(source, source ^ 1) for source in range(count)])


def along_mod(value, step):
    mods = lax.axis_size("mod")
    return lax.ppermute(value, "mod", [(mod, (mod + step) % mods) for mod in range(mods)])


def shards(frames, cycle_label, good_pixel):
    mods = lax.axis_size("mod")
    cycle_dev = CYCLES // mods
    group_cycles = cycle_dev // 2
    mod, frame = lax.axis_index("mod"), lax.axis_index("frame")
    core, chip = frame % 2, frame // 2
    block, pix_count = frames.shape
    per_cycle = pix_count // CYCLES
    frame_count = block * lax.axis_size("frame")
    assert LAG == 8 * block and block == LANES
    place = jnp.stack([core, chip, mod]).astype(jnp.int32)
    half = group_cycles // 2
    parts = [half, group_cycles - half] if half else [group_cycles]

    other = other_core(frames)
    key, counts = rank_pixels(cycle_label, good_pixel)
    (first,) = order_pixels(place, key, frames, other, 0, mods, [group_cycles])
    arrived = [[] for _ in parts]
    counted = [counts]
    for step in range(1, mods):
        sent = order_pixels(place, key, frames, other, step, mods, parts)
        for part, value in zip(arrived, sent):
            part.append(along_mod(value, step))
        counted.append(along_mod(counts, step))
    counts = sum(counted)
    units = [first[None]] + [jnp.stack(part) for part in arrived]
    windows = []
    for own in units:
        two = shifted(own, 2)
        four = shifted(two, 2)
        windows.append(
            (own, two, four, other_pair(own, 1), other_pair(two), other_pair(four, 0))
        )
    whole = None
    swapped = {}
    for phase in range(2):
        for number, count in enumerate(parts):
            offset = sum(parts[:number])
            own, two, four, from_own, from_two, from_four = (
                [(early, offset), (late, 0)]
                for early, late in zip(windows[0], windows[1 + number])
            )
            if phase == 0:
                used, choice = [own, two, from_own, from_two], (0, 1, 2)
            else:
                used, choice = [own, two, four, from_two, from_four], (1, 2, 3)
            sizes = (group_cycles, cycle_dev, offset, count, per_cycle)
            whole, theirs = grams(
                place, counts, whole, used, choice, sizes, phase, frame_count
            )
            swapped[phase, number] = other_core(theirs), (group_cycles, offset, phase * LAG // 2)
    values, spots = zip(*swapped.values())
    return fill(place, whole, list(values), list(spots))


def solution(mesh):
    placed = (P("frame", "mod"), P("mod"), P("mod"))
    return jax.shard_map(
        shards, mesh=mesh, in_specs=placed, out_specs=P("mod", "frame", None), check_vma=False
    )
```

```python
import functools

import jax
import jax.numpy as jnp
from jax import lax
from jax.experimental import pallas as pl
from jax.experimental.pallas import tpu as pltpu
from jax.sharding import PartitionSpec as P

CYCLES = 16
LAG = 1024
LANES = 128
SUBLANES = 8
PACKED = 16
CHUNK = 256
VMEM_LIMIT = 24 * 1024 * 1024

TIES = {
    "z2": ("z0",),
    "w0": ("z1",),
    "z3": ("z2",),
    "w1": ("w0",),
    "w2": ("z3",),
    "w3": ("w1",),
    "x2": ("x0", "o0"),
    "v0": ("x1",),
    "x3": ("x2", "o1"),
    "v1": ("v0",),
    "v2": ("x3",),
    "v3": ("v1",),
    "o1": ("y1",),
    "g00": ("v1",),
    "g01": ("w3", "v1"),
}
OWN_SPLIT = True

SMEM_SPEC = pl.BlockSpec(memory_space=pltpu.SMEM)
VMEM_SPEC = pl.BlockSpec(memory_space=pltpu.VMEM)
HBM_SPEC = pl.BlockSpec(memory_space=pltpu.HBM)
ANY_SPEC = pl.BlockSpec(memory_space=pl.ANY)

dot = functools.partial(jnp.dot, preferred_element_type=jnp.float32)


def params():
    return pltpu.CompilerParams(vmem_limit_bytes=VMEM_LIMIT)


def estimate(flops, moved):
    return pl.CostEstimate(flops=flops, bytes_accessed=moved, transcendentals=0)


def ones_where(condition):
    return jnp.where(condition, 1.0, 0.0).astype(jnp.bfloat16)


def iota(shape, dimension):
    return lax.broadcasted_iota(jnp.int32, shape, dimension)


def rank_kernel(label_ref, frames_hbm, key_ref, counts_ref, frames_ref, sem):
    copy = pltpu.make_async_copy(frames_hbm, frames_ref, sem)
    copy.start()
    chunks = label_ref.shape[0] // CHUNK
    rows = chunks * CYCLES
    up, across = iota((rows, rows), 0), iota((rows, rows), 1)
    same = lax.rem(up, CYCLES) == lax.rem(across, CYCLES)
    chunk_before = ones_where(same & (across < up))
    before = ones_where(iota((CHUNK, CHUNK), 0) < iota((CHUNK, CHUNK), 1))
    of_cycle = ones_where(iota((CYCLES, rows), 0) == lax.rem(iota((CYCLES, rows), 1), CYCLES))
    cycle_at = iota((CYCLES, CHUNK), 0)
    labels = [label_ref[pl.ds(at * CHUNK, CHUNK)].reshape(1, CHUNK) for at in range(chunks)]
    used = jnp.concatenate([jnp.where(one == cycle_at, 1.0, 0.0) for one in labels], axis=0)
    member = used.astype(jnp.bfloat16)
    earlier = dot(chunk_before, member).astype(jnp.bfloat16)
    rank = dot(member, before) + dot(earlier, jnp.ones((CHUNK, CHUNK), jnp.bfloat16))
    key_ref[...] = jnp.where(used > 0.0, rank, -1.0)
    per_lane = dot(of_cycle, member).astype(jnp.bfloat16)
    counts_ref[...] = dot(per_lane, jnp.ones((CHUNK, LANES), jnp.bfloat16))
    copy.wait()


def rank_pixels(label, frames):
    rows = label.shape[0] // CHUNK * CYCLES
    return pl.pallas_call(
        rank_kernel,
        out_shape=[
            jax.ShapeDtypeStruct((rows, CHUNK), jnp.float32),
            jax.ShapeDtypeStruct((CYCLES, LANES), jnp.float32),
            jax.ShapeDtypeStruct(frames.shape, frames.dtype),
        ],
        in_specs=[VMEM_SPEC, HBM_SPEC],
        out_specs=[VMEM_SPEC] * 3,
        scratch_shapes=[pltpu.SemaphoreType.DMA],
        compiler_params=params(),
        cost_estimate=estimate(6 * rows * CHUNK * CHUNK, 8 * label.shape[0]),
    )(label, pltpu.with_memory_space_constraint(frames, pltpu.HBM))


def order_kernel(place_ref, key_ref, *rest, step, mods, parts, joined):
    rest = list(rest)
    core, mod = place_ref[0], place_ref[2]
    if joined:
        frames_ref = rest.pop(0)
    else:
        own_ref, other_ref, frames_ref = rest.pop(0), rest.pop(0), rest.pop()
        block = own_ref.shape[0]
        frames_ref[pl.ds(pl.multiple_of(core * block, block), block), :] = own_ref[...]
        frames_ref[pl.ds(pl.multiple_of((1 - core) * block, block), block), :] = other_ref[...]
    frames = frames_ref[...]
    all_ref, part_refs = rest[0], rest[1:]
    chunks = key_ref.shape[0] // CYCLES
    per_cycle = frames.shape[1] // CYCLES
    first_cycle = (lax.rem(mod + step, mods) * 2 + core) * sum(parts)
    slots = [
        (iota((PACKED, CHUNK), 0) + first).astype(jnp.float32).astype(jnp.bfloat16)
        for first in range(0, per_cycle, PACKED)
    ]
    one = jnp.ones((PACKED, CHUNK), jnp.bfloat16)
    zero = jnp.zeros((PACKED, CHUNK), jnp.bfloat16)
    spots = [(number, at) for number, part in enumerate(parts) for at in range(part)]
    for cycle, (number, at) in enumerate(spots):
        tiles = []
        for chunk in range(chunks):
            key = key_ref[pl.ds(chunk * CYCLES + first_cycle + cycle, 1), :]
            key = jnp.broadcast_to(key, (PACKED, CHUNK)).astype(jnp.bfloat16)
            tiles.append(
                jnp.concatenate([jnp.where(key == slot, one, zero) for slot in slots], axis=0)
            )
        picked = lax.dot_general(
            jnp.concatenate(tiles, axis=1),
            frames,
            (((1,), (1,)), ((), ())),
            preferred_element_type=jnp.float32,
        ).astype(jnp.bfloat16)
        all_ref[cycle * per_cycle : (cycle + 1) * per_cycle, :] = picked
        if part_refs:
            part_refs[number][at * per_cycle : (at + 1) * per_cycle, :] = picked


def order_pixels(place, key, frames, step, mods, parts, split):
    joined = len(frames) == 1
    chip_block = frames[0].shape[0] * (1 if joined else 2)
    pix_count = frames[0].shape[1]
    per_cycle = pix_count // CYCLES
    counts = [sum(parts)] + (list(parts) if split else [])
    out_shape = [
        jax.ShapeDtypeStruct((count * per_cycle, chip_block), jnp.bfloat16) for count in counts
    ]
    if not joined:
        out_shape.append(jax.ShapeDtypeStruct((chip_block, pix_count), jnp.bfloat16))
    return pl.pallas_call(
        functools.partial(order_kernel, step=step, mods=mods, parts=parts, joined=joined),
        out_shape=out_shape,
        in_specs=[SMEM_SPEC] + [VMEM_SPEC] * (1 + len(frames)),
        out_specs=[VMEM_SPEC] * len(out_shape),
        compiler_params=params(),
        cost_estimate=estimate(
            2 * sum(parts) * per_cycle * pix_count * chip_block, 2 * pix_count * chip_block
        ),
    )(place, key, *frames)


def gram_kernel(place_ref, counts_ref, *rest, layout, choice, frame_count, group, offset, count, phase, spots, chained):
    rest = list(rest)
    windows = [[(rest.pop(0), first) for first in pieces] for pieces in layout]
    ready_refs = [rest.pop(0) for _ in spots]
    if chained:
        rest.pop(0)
    out_ref, theirs_ref, mine_ref, gram, later, earlier, sems, fill_sems = rest
    core, chip, mod = place_ref[0], place_ref[1], place_ref[2]
    fills = fill_copies(core, ready_refs, spots, out_ref, fill_sems)
    for copy in fills:
        copy.start()
    _, block, lags = theirs_ref.shape
    chip_block = 2 * block
    per_cycle = CHUNK
    lane, sublane = iota((SUBLANES, LANES), 1), iota((SUBLANES, LANES), 0)
    tiles = lags // LANES
    stores = []
    for cycle in range(count):

        def rows_of(number):
            return jnp.concatenate(
                [
                    ref[source, (first + cycle) * per_cycle : (first + cycle + 1) * per_cycle, :]
                    for ref, first in windows[number]
                    for source in range(ref.shape[0])
                ],
                axis=0,
            )

        columns = [rows_of(number) for number in range(len(windows))]
        own = columns[0]
        at, even, odd = choice
        chosen = jnp.where(lax.rem(chip, 2) == 0, columns[even], columns[odd])
        columns = [
            value
            for number, value in enumerate(columns)
            if number not in (even, odd) and (number or phase == 0)
        ]
        columns.insert(at, chosen)
        whole = jnp.concatenate(columns, axis=1)
        depth, width = whole.shape
        own_rows = own.T
        gram[cycle] = dot(own_rows, whole)
        sums = dot(jnp.ones((PACKED, depth), jnp.bfloat16), whole)[:SUBLANES]
        frame_at = chip * chip_block + phase * lags + iota((SUBLANES, width), 1)
        later[cycle] = jnp.where(frame_at < frame_count, 1.0 / sums, 0.0)
        label = (mod * 2 + core) * group + offset + cycle
        total = counts_ref[pl.ds(label, 1), :]
        earlier[cycle] = total / dot(own_rows, jnp.ones((depth, LANES), jnp.bfloat16))
        for target, position in ((theirs_ref, 1 - core), (mine_ref, core)):
            base = pl.multiple_of(position * block, block)
            for first in range(0, block, SUBLANES):
                factor = earlier[cycle, pl.ds(base + first, SUBLANES), :]
                kept = lane + sublane < LANES - first
                turned = lax.rem(lane + sublane + first, LANES)
                rolled = []
                for tile in range(tiles + 1):
                    column = pl.multiple_of(base + tile * LANES, LANES)
                    value = gram[cycle, pl.ds(base + first, SUBLANES), pl.ds(column, LANES)]
                    value = value * factor * later[cycle, :, pl.ds(column, LANES)]
                    rolled.append(
                        jnp.take_along_axis(value, turned, axis=1, mode="promise_in_bounds")
                    )
                for tile in range(tiles):
                    target[
                        cycle, first : first + SUBLANES, tile * LANES : (tile + 1) * LANES
                    ] = jnp.where(kept, rolled[tile], rolled[tile + 1])
        store = pltpu.make_async_copy(
            mine_ref.at[cycle],
            out_ref.at[core * group + offset + cycle, :, pl.ds(phase * lags, lags)],
            sems.at[cycle],
        )
        store.start()
        stores.append(store)
    for copy in stores + fills:
        copy.wait()


def grams(place, counts, whole, windows, choice, sizes, phase, frame_count, ready):
    group_cycles, cycle_dev, offset, count = sizes
    flat = [piece for pieces in windows for piece, _ in pieces]
    chip_block = flat[0].shape[-1]
    block = chip_block // 2
    depth = sum(piece.shape[0] for piece, _ in windows[0]) * CHUNK
    lags = LAG // 2
    width = lags + chip_block
    kernel = functools.partial(
        gram_kernel,
        layout=[[first for _, first in pieces] for pieces in windows],
        choice=choice,
        frame_count=frame_count,
        group=group_cycles,
        offset=offset,
        count=count,
        phase=phase,
        spots=[spot for _, spot in ready],
        chained=whole is not None,
    )
    operands = [place, counts] + flat + [part for part, _ in ready]
    in_specs = [SMEM_SPEC] + [VMEM_SPEC] * (1 + len(flat)) + [ANY_SPEC] * len(ready)
    aliases = {}
    if whole is not None:
        aliases = {len(operands): 0}
        operands.append(whole)
        in_specs.append(ANY_SPEC)
    return pl.pallas_call(
        kernel,
        out_shape=[
            jax.ShapeDtypeStruct((cycle_dev, block, LAG), jnp.float32),
            jax.ShapeDtypeStruct((count, block, lags), jnp.float32),
        ],
        in_specs=in_specs,
        out_specs=[ANY_SPEC, VMEM_SPEC],
        scratch_shapes=[
            pltpu.VMEM((count, block, lags), jnp.float32),
            pltpu.VMEM((count, chip_block, width), jnp.float32),
            pltpu.VMEM((count, SUBLANES, width), jnp.float32),
            pltpu.VMEM((count, chip_block, LANES), jnp.float32),
            pltpu.SemaphoreType.DMA((count,)),
            pltpu.SemaphoreType.DMA((max(1, len(ready)),)),
        ],
        input_output_aliases=aliases,
        compiler_params=params(),
        cost_estimate=estimate(
            2 * count * depth * width * chip_block, 4 * count * chip_block * lags
        ),
    )(*operands)


def fill_copies(core, part_refs, spots, out_ref, sems):
    copies = []
    for number, (part_ref, (group, offset, lag)) in enumerate(zip(part_refs, spots)):
        cycles, _, lags = part_ref.shape
        first = (1 - core) * group + offset
        copies.append(
            pltpu.make_async_copy(
                part_ref,
                out_ref.at[pl.ds(first, cycles), :, pl.ds(lag, lags)],
                sems.at[number],
            )
        )
    return copies


def fill_kernel(place_ref, *rest, spots):
    part_refs, out_ref, sems = rest[: len(spots)], rest[-2], rest[-1]
    copies = fill_copies(place_ref[0], part_refs, spots, out_ref, sems)
    for copy in copies:
        copy.start()
    for copy in copies:
        copy.wait()


def fill(place, whole, ready):
    parts, spots = zip(*ready)
    return pl.pallas_call(
        functools.partial(fill_kernel, spots=spots),
        out_shape=jax.ShapeDtypeStruct(whole.shape, whole.dtype),
        in_specs=[SMEM_SPEC] + [ANY_SPEC] * (len(parts) + 1),
        out_specs=ANY_SPEC,
        scratch_shapes=[pltpu.SemaphoreType.DMA((len(parts),))],
        input_output_aliases={1 + len(parts): 0},
        compiler_params=params(),
        cost_estimate=estimate(0, 8 * sum(part.size for part in parts)),
    )(place, *parts, whole)


def shifted(value, pairs_down):
    step = 2 * pairs_down
    count = lax.axis_size("frame")
    return lax.ppermute(value, "frame", [(source, source - step) for source in range(step, count)])


def other_pair(value, parity=None):
    count = lax.axis_size("frame")
    sources = [at for at in range(count) if parity is None or at // 2 % 2 == parity]
    return lax.ppermute(value, "frame", [(source, source ^ 2) for source in sources])


def other_core(value):
    count = lax.axis_size("frame")
    return lax.ppermute(value, "frame", [(source, source ^ 1) for source in range(count)])


def along_mod(value, step, odd_pairs=False):
    frames, mods = lax.axis_size("frame"), lax.axis_size("mod")
    pairs = [
        (frame * mods + mod, (frame - 2 * odd_pairs) * mods + (mod + step) % mods)
        for frame in range(frames)
        for mod in range(mods)
        if not odd_pairs or frame // 2 % 2
    ]
    return lax.ppermute(value, ("frame", "mod"), pairs)


def shards(frames, cycle_label, good_pixel):
    mods = lax.axis_size("mod")
    cycle_dev = CYCLES // mods
    group_cycles = cycle_dev // 2
    mod, frame = lax.axis_index("mod"), lax.axis_index("frame")
    core, chip = frame % 2, frame // 2
    block, pix_count = frames.shape
    frame_count = block * lax.axis_size("frame")
    assert LAG == 8 * block and block == LANES and pix_count == CYCLES * CHUNK
    place = jnp.stack([core, chip, mod]).astype(jnp.int32)
    half = group_cycles // 2
    parts = [half, group_cycles - half] if half else [group_cycles]
    offsets = [sum(parts[:number]) for number in range(len(parts))]

    halves = len(parts)
    own_units = halves if OWN_SPLIT else 1
    other = other_core(frames)
    used = jnp.where(good_pixel > 0, cycle_label, CYCLES)
    key, counts, own_frames = rank_pixels(used, frames)
    done = {}

    def tied(value, name):
        ties = [get(tie) for tie in TIES.get(name, ()) if known(tie)]
        ties = [tie[0] if isinstance(tie, (list, tuple)) else tie for tie in ties]
        return lax.optimization_barrier((value, *ties))[0] if ties else value

    def known(name):
        limits = dict(g=halves, s=halves, y=halves, k=mods, o=2, c=1)
        return all(int(at) < limits.get(name[0], own_units + halves) for at in name[-1])

    def get(name):
        if name not in done:
            done[name] = make(name[0], name, *(int(at) for at in name[1:]))
        return done[name]

    def make(kind, name, first, second=0):
        if kind == "k":
            joined = [own_frames, other] if first == 0 else [get("k0")[-1]]
            split = halves > 1 and (first > 0 or own_units > 1)
            return order_pixels(place, tied(key, name), joined, first, mods, parts, split)
        if kind == "y":
            at = 1 + first if halves > 1 else 0
            return jnp.stack(
                [along_mod(tied(get(f"k{step}")[at], name), step) for step in range(1, mods)]
            )
        if kind == "c":
            value = tied(counts, name)
            return sum([value] + [along_mod(value, step) for step in range(1, mods)])
        if kind == "u":
            if first >= own_units:
                return get(f"y{first - own_units}")
            return get("k0")[1 + first if own_units > 1 else 0][None]
        if kind == "z":
            return shifted(tied(get(f"u{first}"), name), 2)
        if kind == "w":
            return shifted(tied(get(f"z{first}"), name), 2)
        if kind == "x":
            return other_pair(tied(get(f"z{first}"), name))
        if kind == "v":
            return other_pair(tied(get(f"w{first}"), name), 0)
        if kind == "o":
            if first == 0:
                return other_pair(tied(get("k0")[0], name), 1)[None]
            return jnp.stack(
                [along_mod(tied(get(f"k{step}")[0], name), step, True) for step in range(1, mods)]
            )
        if kind == "s":
            return other_core(get(f"g{first}{second}")[1])
        assert kind == "g"
        phase, part = first, second

        def both(letter):
            early = (get(f"{letter}{part}"), 0) if own_units > 1 else (get(f"{letter}0"), offsets[part])
            return [early, (get(f"{letter}{own_units + part}"), 0)]

        if phase == 0:
            neighbour = [(get(f"o{at}"), offsets[part]) for at in range(2)]
            windows, choice = [both("u"), both("z"), neighbour, both("x")], (1, 2, 3)
        else:
            windows = [both(letter) for letter in "uzwxv"]
            choice = (1, 3, 4)
        before = phase * halves + part - 1
        whole = get(f"g{before // halves}{before % halves}")[0] if before >= 0 else None
        filled = [spot(0, at) for at in range(halves)] if phase and not part else []
        sizes = (group_cycles, cycle_dev, offsets[part], parts[part])
        return grams(
            place, tied(get("c0"), name), whole, windows, choice, sizes, phase, frame_count, filled
        )

    def spot(phase, part):
        return get(f"s{phase}{part}"), (group_cycles, offsets[part], phase * (LAG // 2))

    whole = get(f"g1{halves - 1}")[0]
    return fill(place, whole, [spot(1, part) for part in range(halves)])


def solution(mesh):
    placed = (P("frame", "mod"), P("mod"), P("mod"))
    return jax.shard_map(
        shards, mesh=mesh, in_specs=placed, out_specs=P("mod", "frame", None), check_vma=False
    )
```

```python
import functools

import jax
import jax.numpy as jnp
from jax import lax
from jax.experimental import pallas as pl
from jax.experimental.pallas import tpu as pltpu
from jax.sharding import PartitionSpec as P

CYCLES = 16
LAG = 1024
LANES = 128
SUBLANES = 8
PACKED = 16
BATCH = 64
CHUNK = 256
VMEM_LIMIT = 24 * 1024 * 1024

TIES = {
    "z3": ("x1", "y1", "y0", "z2"),
    "x2": ("x0", "o0", "y1"),
    "v0": ("x1", "k1"),
    "x3": ("x2", "o1"),
    "v1": ("v0", "y1", "o0", "w1"),
    "g00": ("v1",),
    "g01": ("w3", "v1", "v2", "v0"),
    "w3": ("z1",),
    "x1": ("z1", "o0"),
    "w0": ("z0",),
    "y0": ("k1",),
}
OWN_SPLIT = True

SMEM_SPEC = pl.BlockSpec(memory_space=pltpu.SMEM)
VMEM_SPEC = pl.BlockSpec(memory_space=pltpu.VMEM)
HBM_SPEC = pl.BlockSpec(memory_space=pltpu.HBM)
ANY_SPEC = pl.BlockSpec(memory_space=pl.ANY)

dot = functools.partial(jnp.dot, preferred_element_type=jnp.float32)


def params():
    return pltpu.CompilerParams(vmem_limit_bytes=VMEM_LIMIT)


def estimate(flops, moved):
    return pl.CostEstimate(flops=flops, bytes_accessed=moved, transcendentals=0)


def ones_where(condition):
    return jnp.where(condition, 1.0, 0.0).astype(jnp.bfloat16)


def iota(shape, dimension):
    return lax.broadcasted_iota(jnp.int32, shape, dimension)


def rank_kernel(label_ref, frames_hbm, key_ref, counts_ref, frames_ref, sem):
    copy = pltpu.make_async_copy(frames_hbm, frames_ref, sem)
    copy.start()
    chunks = label_ref.shape[0] // CHUNK
    rows = chunks * CYCLES
    up, across = iota((rows, rows), 0), iota((rows, rows), 1)
    same = lax.rem(up, CYCLES) == lax.rem(across, CYCLES)
    chunk_before = ones_where(same & (across < up))
    before = ones_where(iota((CHUNK, CHUNK), 0) < iota((CHUNK, CHUNK), 1))
    of_cycle = ones_where(iota((CYCLES, rows), 0) == lax.rem(iota((CYCLES, rows), 1), CYCLES))
    cycle_at = iota((CYCLES, CHUNK), 0)
    labels = [label_ref[pl.ds(at * CHUNK, CHUNK)].reshape(1, CHUNK) for at in range(chunks)]
    used = jnp.concatenate([jnp.where(one == cycle_at, 1.0, 0.0) for one in labels], axis=0)
    member = used.astype(jnp.bfloat16)
    earlier = dot(chunk_before, member).astype(jnp.bfloat16)
    rank = dot(member, before) + dot(earlier, jnp.ones((CHUNK, CHUNK), jnp.bfloat16))
    key_ref[...] = jnp.where(used > 0.0, rank, -1.0)
    per_lane = dot(of_cycle, member).astype(jnp.bfloat16)
    counts_ref[...] = dot(per_lane, jnp.ones((CHUNK, LANES), jnp.bfloat16))
    copy.wait()


def rank_pixels(label, frames):
    rows = label.shape[0] // CHUNK * CYCLES
    return pl.pallas_call(
        rank_kernel,
        out_shape=[
            jax.ShapeDtypeStruct((rows, CHUNK), jnp.float32),
            jax.ShapeDtypeStruct((CYCLES, LANES), jnp.float32),
            jax.ShapeDtypeStruct(frames.shape, frames.dtype),
        ],
        in_specs=[VMEM_SPEC, HBM_SPEC],
        out_specs=[VMEM_SPEC] * 3,
        scratch_shapes=[pltpu.SemaphoreType.DMA],
        compiler_params=params(),
        cost_estimate=estimate(6 * rows * CHUNK * CHUNK, 8 * label.shape[0]),
    )(label, pltpu.with_memory_space_constraint(frames, pltpu.HBM))


def order_kernel(place_ref, key_ref, counts_ref, *rest, step, mods, parts, joined):
    rest = list(rest)
    core, mod = place_ref[0], place_ref[2]
    if joined:
        frames_ref = rest.pop(0)
    else:
        own_ref, other_ref, frames_ref = rest.pop(0), rest.pop(0), rest.pop()
        block = own_ref.shape[0]
        frames_ref[pl.ds(pl.multiple_of(core * block, block), block), :] = own_ref[...]
        frames_ref[pl.ds(pl.multiple_of((1 - core) * block, block), block), :] = other_ref[...]
    frames = frames_ref[...]
    all_ref, part_refs = rest[0], rest[1:]
    chunks = key_ref.shape[0] // CYCLES
    per_cycle = frames.shape[1] // CYCLES
    first_cycle = (lax.rem(mod + step, mods) * 2 + core) * sum(parts)
    if step:
        row = parts[0] * per_cycle
        sent = jnp.concatenate([counts_ref[...]] * (frames.shape[0] // LANES), axis=1)
        part_refs[0][row : row + CYCLES, :] = sent.astype(jnp.bfloat16)
    slots = [
        (iota((PACKED, CHUNK), 0) + first).astype(jnp.float32).astype(jnp.bfloat16)
        for first in range(0, per_cycle, PACKED)
    ]
    one = jnp.ones((PACKED, CHUNK), jnp.bfloat16)
    zero = jnp.zeros((PACKED, CHUNK), jnp.bfloat16)
    spots = [(number, at) for number, part in enumerate(parts) for at in range(part)]
    for cycle, (number, at) in enumerate(spots):
        tiles = []
        for chunk in range(chunks):
            key = key_ref[pl.ds(chunk * CYCLES + first_cycle + cycle, 1), :]
            key = jnp.broadcast_to(key, (PACKED, CHUNK)).astype(jnp.bfloat16)
            tiles.append(
                jnp.concatenate([jnp.where(key == slot, one, zero) for slot in slots], axis=0)
            )
        picked = lax.dot_general(
            jnp.concatenate(tiles, axis=1),
            frames,
            (((1,), (1,)), ((), ())),
            preferred_element_type=jnp.float32,
        ).astype(jnp.bfloat16)
        all_ref[cycle * per_cycle : (cycle + 1) * per_cycle, :] = picked
        if part_refs:
            part_refs[number][at * per_cycle : (at + 1) * per_cycle, :] = picked


def order_pixels(place, key, counts, frames, step, mods, parts, split):
    joined = len(frames) == 1
    chip_block = frames[0].shape[0] * (1 if joined else 2)
    pix_count = frames[0].shape[1]
    per_cycle = pix_count // CYCLES
    heights = [part * per_cycle for part in [sum(parts)] + (list(parts) if split else [])]
    if step:
        heights[1] += CYCLES
    out_shape = [jax.ShapeDtypeStruct((height, chip_block), jnp.bfloat16) for height in heights]
    if not joined:
        out_shape.append(jax.ShapeDtypeStruct((chip_block, pix_count), jnp.bfloat16))
    return pl.pallas_call(
        functools.partial(order_kernel, step=step, mods=mods, parts=parts, joined=joined),
        out_shape=out_shape,
        in_specs=[SMEM_SPEC] + [VMEM_SPEC] * (2 + len(frames)),
        out_specs=[VMEM_SPEC] * len(out_shape),
        compiler_params=params(),
        cost_estimate=estimate(
            2 * sum(parts) * per_cycle * pix_count * chip_block, 2 * pix_count * chip_block
        ),
    )(place, key, counts, *frames)


def gram_kernel(place_ref, counts_ref, sent_ref, *rest, layout, choice, frame_count, group, offset, count, phase, spots, chained):
    rest = list(rest)
    windows = [[(rest.pop(0), first) for first in pieces] for pieces in layout]
    ready_refs = [rest.pop(0) for _ in spots]
    if chained:
        rest.pop(0)
    out_ref, theirs_ref, mine_ref, gram, later, earlier, sems, fill_sems = rest
    core, chip, mod = place_ref[0], place_ref[1], place_ref[2]
    fills = fill_copies(core, ready_refs, spots, out_ref, fill_sems)
    for copy in fills:
        copy.start()
    _, block, lags = theirs_ref.shape
    chip_block = 2 * block
    per_cycle = CHUNK
    lane, sublane = iota((SUBLANES, LANES), 1), iota((SUBLANES, LANES), 0)
    tiles = lags // LANES
    stores = []
    for cycle in range(count):

        def rows_of(number):
            return jnp.concatenate(
                [
                    ref[source, (first + cycle) * per_cycle : (first + cycle + 1) * per_cycle, :]
                    for ref, first in windows[number]
                    for source in range(ref.shape[0])
                ],
                axis=0,
            )

        columns = [rows_of(number) for number in range(len(windows))]
        own = columns[0]
        at, even, odd = choice
        chosen = jnp.where(lax.rem(chip, 2) == 0, columns[even], columns[odd])
        columns = [
            value
            for number, value in enumerate(columns)
            if number not in (even, odd) and (number or phase == 0)
        ]
        columns.insert(at, chosen)
        whole = jnp.concatenate(columns, axis=1)
        depth, width = whole.shape
        own_rows = own.T
        gram[cycle] = dot(own_rows, whole)
        sums = dot(jnp.ones((PACKED, depth), jnp.bfloat16), whole)[:SUBLANES]
        frame_at = chip * chip_block + phase * lags + iota((SUBLANES, width), 1)
        later[cycle] = jnp.where(frame_at < frame_count, 1.0 / sums, 0.0)
        label = (mod * 2 + core) * group + offset + cycle
        total = counts_ref[pl.ds(label, 1), :]
        for source in range(sent_ref.shape[0]):
            sent = sent_ref[source, sent_ref.shape[1] - CYCLES :, :LANES].astype(jnp.float32)
            total += jnp.sum(
                jnp.where(iota((CYCLES, LANES), 0) == label, sent, 0.0), axis=0, keepdims=True
            )
        earlier[cycle] = total / dot(own_rows, jnp.ones((depth, LANES), jnp.bfloat16))
        for target, position in ((theirs_ref, 1 - core), (mine_ref, core)):
            base = pl.multiple_of(position * block, block)
            scales = [
                later[cycle, :, pl.ds(pl.multiple_of(base + tile * LANES, LANES), LANES)]
                for tile in range(tiles + 1)
            ]
            for batch in range(0, block, BATCH):
                results = []
                for first in range(batch, batch + BATCH, SUBLANES):
                    factor = earlier[cycle, pl.ds(base + first, SUBLANES), :]
                    kept = lane + sublane < LANES - first
                    turned = lax.rem(lane + sublane + first, LANES)
                    rolled = []
                    for tile in range(tiles + 1):
                        column = pl.multiple_of(base + tile * LANES, LANES)
                        value = gram[cycle, pl.ds(base + first, SUBLANES), pl.ds(column, LANES)]
                        value = value * factor * scales[tile]
                        rolled.append(
                            jnp.take_along_axis(value, turned, axis=1, mode="promise_in_bounds")
                        )
                    for tile in range(tiles):
                        results.append(jnp.where(kept, rolled[tile], rolled[tile + 1]))
                at = 0
                for first in range(batch, batch + BATCH, SUBLANES):
                    for tile in range(tiles):
                        target[
                            cycle, first : first + SUBLANES, tile * LANES : (tile + 1) * LANES
                        ] = results[at]
                        at += 1
        store = pltpu.make_async_copy(
            mine_ref.at[cycle],
            out_ref.at[core * group + offset + cycle, :, pl.ds(phase * lags, lags)],
            sems.at[cycle],
        )
        store.start()
        stores.append(store)
    for copy in stores + fills:
        copy.wait()


def grams(place, counts, sent, whole, windows, choice, sizes, phase, frame_count, ready):
    group_cycles, cycle_dev, offset, count = sizes
    flat = [piece for pieces in windows for piece, _ in pieces]
    chip_block = flat[0].shape[-1]
    block = chip_block // 2
    depth = sum(piece.shape[0] for piece, _ in windows[0]) * CHUNK
    lags = LAG // 2
    width = lags + chip_block
    kernel = functools.partial(
        gram_kernel,
        layout=[[first for _, first in pieces] for pieces in windows],
        choice=choice,
        frame_count=frame_count,
        group=group_cycles,
        offset=offset,
        count=count,
        phase=phase,
        spots=[spot for _, spot in ready],
        chained=whole is not None,
    )
    operands = [place, counts, sent] + flat + [part for part, _ in ready]
    in_specs = [SMEM_SPEC] + [VMEM_SPEC] * (2 + len(flat)) + [ANY_SPEC] * len(ready)
    aliases = {}
    if whole is not None:
        aliases = {len(operands): 0}
        operands.append(whole)
        in_specs.append(ANY_SPEC)
    return pl.pallas_call(
        kernel,
        out_shape=[
            jax.ShapeDtypeStruct((cycle_dev, block, LAG), jnp.float32),
            jax.ShapeDtypeStruct((count, block, lags), jnp.float32),
        ],
        in_specs=in_specs,
        out_specs=[ANY_SPEC, VMEM_SPEC],
        scratch_shapes=[
            pltpu.VMEM((count, block, lags), jnp.float32),
            pltpu.VMEM((count, chip_block, width), jnp.float32),
            pltpu.VMEM((count, SUBLANES, width), jnp.float32),
            pltpu.VMEM((count, chip_block, LANES), jnp.float32),
            pltpu.SemaphoreType.DMA((count,)),
            pltpu.SemaphoreType.DMA((max(1, len(ready)),)),
        ],
        input_output_aliases=aliases,
        compiler_params=params(),
        cost_estimate=estimate(
            2 * count * depth * width * chip_block, 4 * count * chip_block * lags
        ),
    )(*operands)


def fill_copies(core, part_refs, spots, out_ref, sems):
    copies = []
    for number, (part_ref, (group, offset, lag)) in enumerate(zip(part_refs, spots)):
        cycles, _, lags = part_ref.shape
        first = (1 - core) * group + offset
        copies.append(
            pltpu.make_async_copy(
                part_ref,
                out_ref.at[pl.ds(first, cycles), :, pl.ds(lag, lags)],
                sems.at[number],
            )
        )
    return copies


def fill_kernel(place_ref, *rest, spots):
    part_refs, out_ref, sems = rest[: len(spots)], rest[-2], rest[-1]
    copies = fill_copies(place_ref[0], part_refs, spots, out_ref, sems)
    for copy in copies:
        copy.start()
    for copy in copies:
        copy.wait()


def fill(place, whole, ready):
    parts, spots = zip(*ready)
    return pl.pallas_call(
        functools.partial(fill_kernel, spots=spots),
        out_shape=jax.ShapeDtypeStruct(whole.shape, whole.dtype),
        in_specs=[SMEM_SPEC] + [ANY_SPEC] * (len(parts) + 1),
        out_specs=ANY_SPEC,
        scratch_shapes=[pltpu.SemaphoreType.DMA((len(parts),))],
        input_output_aliases={1 + len(parts): 0},
        compiler_params=params(),
        cost_estimate=estimate(0, 8 * sum(part.size for part in parts)),
    )(place, *parts, whole)


def shifted(value, pairs_down):
    step = 2 * pairs_down
    count = lax.axis_size("frame")
    return lax.ppermute(value, "frame", [(source, source - step) for source in range(step, count)])


def other_pair(value, parity=None):
    count = lax.axis_size("frame")
    sources = [at for at in range(count) if parity is None or at // 2 % 2 == parity]
    return lax.ppermute(value, "frame", [(source, source ^ 2) for source in sources])


def other_core(value):
    count = lax.axis_size("frame")
    return lax.ppermute(value, "frame", [(source, source ^ 1) for source in range(count)])


def along_mod(value, step, odd_pairs=False):
    frames, mods = lax.axis_size("frame"), lax.axis_size("mod")
    pairs = [
        (frame * mods + mod, (frame - 2 * odd_pairs) * mods + (mod + step) % mods)
        for frame in range(frames)
        for mod in range(mods)
        if not odd_pairs or frame // 2 % 2
    ]
    return lax.ppermute(value, ("frame", "mod"), pairs)


def shards(frames, cycle_label, good_pixel):
    mods = lax.axis_size("mod")
    cycle_dev = CYCLES // mods
    group_cycles = cycle_dev // 2
    mod, frame = lax.axis_index("mod"), lax.axis_index("frame")
    core, chip = frame % 2, frame // 2
    block, pix_count = frames.shape
    frame_count = block * lax.axis_size("frame")
    assert LAG == 8 * block and block == LANES and pix_count == CYCLES * CHUNK
    place = jnp.stack([core, chip, mod]).astype(jnp.int32)
    half = group_cycles // 2
    parts = [half, group_cycles - half] if half else [group_cycles]
    offsets = [sum(parts[:number]) for number in range(len(parts))]

    halves = len(parts)
    own_units = halves if OWN_SPLIT else 1
    other = other_core(frames)
    used = jnp.where(good_pixel > 0, cycle_label, CYCLES)
    key, counts, own_frames = rank_pixels(used, frames)
    done = {}

    def tied(value, name):
        ties = [get(tie) for tie in TIES.get(name, ()) if known(tie)]
        ties = [tie[0] if isinstance(tie, (list, tuple)) else tie for tie in ties]
        return lax.optimization_barrier((value, *ties))[0] if ties else value

    def known(name):
        limits = dict(g=halves, s=halves, y=halves, k=mods, o=2)
        return all(int(at) < limits.get(name[0], own_units + halves) for at in name[-1])

    def get(name):
        if name not in done:
            done[name] = make(name[0], name, *(int(at) for at in name[1:]))
        return done[name]

    def make(kind, name, first, second=0):
        if kind == "k":
            joined = [own_frames, other] if first == 0 else [get("k0")[-1]]
            split = first > 0 or own_units > 1
            return order_pixels(place, tied(key, name), counts, joined, first, mods, parts, split)
        if kind == "y":
            return jnp.stack(
                [along_mod(tied(get(f"k{step}")[1 + first], name), step) for step in range(1, mods)]
            )
        if kind == "u":
            if first >= own_units:
                return get(f"y{first - own_units}")
            return get("k0")[1 + first if own_units > 1 else 0][None]
        if kind == "z":
            return shifted(tied(get(f"u{first}"), name), 2)
        if kind == "w":
            return shifted(tied(get(f"z{first}"), name), 2)
        if kind == "x":
            return other_pair(tied(get(f"z{first}"), name))
        if kind == "v":
            return other_pair(tied(get(f"w{first}"), name), 0)
        if kind == "o":
            if first == 0:
                return other_pair(tied(get("k0")[0], name), 1)[None]
            return jnp.stack(
                [along_mod(tied(get(f"k{step}")[0], name), step, True) for step in range(1, mods)]
            )
        if kind == "s":
            return other_core(get(f"g{first}{second}")[1])
        assert kind == "g"
        phase, part = first, second

        def both(letter):
            early = (get(f"{letter}{part}"), 0) if own_units > 1 else (get(f"{letter}0"), offsets[part])
            return [early, (get(f"{letter}{own_units + part}"), 0)]

        if phase == 0:
            neighbour = [(get(f"o{at}"), offsets[part]) for at in range(2)]
            windows, choice = [both("u"), both("z"), neighbour, both("x")], (1, 2, 3)
        else:
            windows = [both(letter) for letter in "uzwxv"]
            choice = (1, 3, 4)
        before = phase * halves + part - 1
        whole = get(f"g{before // halves}{before % halves}")[0] if before >= 0 else None
        filled = [spot(0, at) for at in range(halves)] if phase and not part else []
        sizes = (group_cycles, cycle_dev, offsets[part], parts[part])
        return grams(
            place, tied(counts, name), get(f"u{own_units}"), whole, windows, choice, sizes, phase, frame_count, filled
        )

    def spot(phase, part):
        return get(f"s{phase}{part}"), (group_cycles, offsets[part], phase * (LAG // 2))

    whole = get(f"g1{halves - 1}")[0]
    return fill(place, whole, [spot(1, part) for part in range(halves)])


def solution(mesh):
    placed = (P("frame", "mod"), P("mod"), P("mod"))
    return jax.shard_map(
        shards, mesh=mesh, in_specs=placed, out_specs=P("mod", "frame", None), check_vma=False
    )
```

```python
import functools

import jax
import jax.numpy as jnp
from jax import lax
from jax.experimental import pallas as pl
from jax.experimental.pallas import tpu as pltpu
from jax.sharding import PartitionSpec as P

CYCLES = 16
LAG = 1024
LANES = 128
SUBLANES = 8
PACKED = 16
BATCH = 64
CHUNK = 256
VMEM_LIMIT = 24 * 1024 * 1024

TIES = {
    "z3": ("x1", "y1", "y0", "z2"),
    "x2": ("x0", "o0", "y1"),
    "v0": ("x1", "k1"),
    "x3": ("x2", "o1"),
    "v1": ("v0", "y1", "o0", "w1"),
    "g00": ("v1",),
    "g01": ("w3", "v1", "v2", "v0"),
    "w3": ("z1",),
    "x1": ("z1", "o0"),
    "w0": ("z0",),
    "y0": ("k1",),
}
OWN_SPLIT = True

SMEM_SPEC = pl.BlockSpec(memory_space=pltpu.SMEM)
VMEM_SPEC = pl.BlockSpec(memory_space=pltpu.VMEM)
HBM_SPEC = pl.BlockSpec(memory_space=pltpu.HBM)
ANY_SPEC = pl.BlockSpec(memory_space=pl.ANY)

dot = functools.partial(jnp.dot, preferred_element_type=jnp.float32)


def params():
    return pltpu.CompilerParams(vmem_limit_bytes=VMEM_LIMIT)


def estimate(flops, moved):
    return pl.CostEstimate(flops=flops, bytes_accessed=moved, transcendentals=0)


def ones_where(condition):
    return jnp.where(condition, 1.0, 0.0).astype(jnp.bfloat16)


def iota(shape, dimension):
    return lax.broadcasted_iota(jnp.int32, shape, dimension)


def rank_kernel(label_ref, frames_hbm, key_ref, counts_ref, frames_ref, sem):
    copy = pltpu.make_async_copy(frames_hbm, frames_ref, sem)
    copy.start()
    chunks = label_ref.shape[0] // CHUNK
    rows = chunks * CYCLES
    up, across = iota((rows, rows), 0), iota((rows, rows), 1)
    same = lax.rem(up, CYCLES) == lax.rem(across, CYCLES)
    chunk_before = ones_where(same & (across < up))
    before = ones_where(iota((CHUNK, CHUNK), 0) < iota((CHUNK, CHUNK), 1))
    of_cycle = ones_where(iota((CYCLES, rows), 0) == lax.rem(iota((CYCLES, rows), 1), CYCLES))
    cycle_at = iota((CYCLES, CHUNK), 0)
    labels = [label_ref[pl.ds(at * CHUNK, CHUNK)].reshape(1, CHUNK) for at in range(chunks)]
    used = jnp.concatenate([jnp.where(one == cycle_at, 1.0, 0.0) for one in labels], axis=0)
    member = used.astype(jnp.bfloat16)
    earlier = dot(chunk_before, member).astype(jnp.bfloat16)
    rank = dot(member, before) + dot(earlier, jnp.ones((CHUNK, CHUNK), jnp.bfloat16))
    key_ref[...] = jnp.where(used > 0.0, rank, -1.0)
    per_lane = dot(of_cycle, member).astype(jnp.bfloat16)
    counts_ref[...] = dot(per_lane, jnp.ones((CHUNK, LANES), jnp.bfloat16))
    copy.wait()


def rank_pixels(label, frames):
    rows = label.shape[0] // CHUNK * CYCLES
    return pl.pallas_call(
        rank_kernel,
        out_shape=[
            jax.ShapeDtypeStruct((rows, CHUNK), jnp.float32),
            jax.ShapeDtypeStruct((CYCLES, LANES), jnp.float32),
            jax.ShapeDtypeStruct(frames.shape, frames.dtype),
        ],
        in_specs=[VMEM_SPEC, HBM_SPEC],
        out_specs=[VMEM_SPEC] * 3,
        scratch_shapes=[pltpu.SemaphoreType.DMA],
        compiler_params=params(),
        cost_estimate=estimate(6 * rows * CHUNK * CHUNK, 8 * label.shape[0]),
    )(label, pltpu.with_memory_space_constraint(frames, pltpu.HBM))


def order_kernel(place_ref, key_ref, counts_ref, *rest, step, mods, parts, joined):
    rest = list(rest)
    core, mod = place_ref[0], place_ref[2]
    if joined:
        frames_ref = rest.pop(0)
    else:
        own_ref, other_ref, frames_ref = rest.pop(0), rest.pop(0), rest.pop()
        block = own_ref.shape[0]
        frames_ref[pl.ds(pl.multiple_of(core * block, block), block), :] = own_ref[...]
        frames_ref[pl.ds(pl.multiple_of((1 - core) * block, block), block), :] = other_ref[...]
    frames = frames_ref[...]
    all_ref, part_refs = rest[0], rest[1:]
    chunks = key_ref.shape[0] // CYCLES
    per_cycle = frames.shape[1] // CYCLES
    first_cycle = (lax.rem(mod + step, mods) * 2 + core) * sum(parts)
    if step:
        row = parts[0] * per_cycle
        sent = jnp.concatenate([counts_ref[...]] * (frames.shape[0] // LANES), axis=1)
        part_refs[0][row : row + CYCLES, :] = sent.astype(jnp.bfloat16)
    slots = [
        (iota((PACKED, CHUNK), 0) + first).astype(jnp.float32).astype(jnp.bfloat16)
        for first in range(0, per_cycle, PACKED)
    ]
    one = jnp.ones((PACKED, CHUNK), jnp.bfloat16)
    zero = jnp.zeros((PACKED, CHUNK), jnp.bfloat16)
    spots = [(number, at) for number, part in enumerate(parts) for at in range(part)]
    for cycle, (number, at) in enumerate(spots):
        tiles = []
        for chunk in range(chunks):
            key = key_ref[pl.ds(chunk * CYCLES + first_cycle + cycle, 1), :]
            key = jnp.broadcast_to(key, (PACKED, CHUNK)).astype(jnp.bfloat16)
            tiles.append(
                jnp.concatenate([jnp.where(key == slot, one, zero) for slot in slots], axis=0)
            )
        picked = lax.dot_general(
            jnp.concatenate(tiles, axis=1),
            frames,
            (((1,), (1,)), ((), ())),
            preferred_element_type=jnp.float32,
        ).astype(jnp.bfloat16)
        all_ref[cycle * per_cycle : (cycle + 1) * per_cycle, :] = picked
        if part_refs:
            part_refs[number][at * per_cycle : (at + 1) * per_cycle, :] = picked


def order_pixels(place, key, counts, frames, step, mods, parts, split):
    joined = len(frames) == 1
    chip_block = frames[0].shape[0] * (1 if joined else 2)
    pix_count = frames[0].shape[1]
    per_cycle = pix_count // CYCLES
    heights = [part * per_cycle for part in [sum(parts)] + (list(parts) if split else [])]
    if step:
        heights[1] += CYCLES
    out_shape = [jax.ShapeDtypeStruct((height, chip_block), jnp.bfloat16) for height in heights]
    if not joined:
        out_shape.append(jax.ShapeDtypeStruct((chip_block, pix_count), jnp.bfloat16))
    return pl.pallas_call(
        functools.partial(order_kernel, step=step, mods=mods, parts=parts, joined=joined),
        out_shape=out_shape,
        in_specs=[SMEM_SPEC] + [VMEM_SPEC] * (2 + len(frames)),
        out_specs=[VMEM_SPEC] * len(out_shape),
        compiler_params=params(),
        cost_estimate=estimate(
            2 * sum(parts) * per_cycle * pix_count * chip_block, 2 * pix_count * chip_block
        ),
    )(place, key, counts, *frames)


def gram_kernel(place_ref, counts_ref, sent_ref, *rest, layout, choice, frame_count, group, offset, count, phase, spots, chained):
    rest = list(rest)
    windows = [[(rest.pop(0), first) for first in pieces] for pieces in layout]
    ready_refs = [rest.pop(0) for _ in spots]
    if chained:
        rest.pop(0)
    out_ref, theirs_ref, mine_ref, gram, later, earlier, sems, fill_sems = rest
    core, chip, mod = place_ref[0], place_ref[1], place_ref[2]
    fills = fill_copies(core, ready_refs, spots, out_ref, fill_sems)
    for copy in fills:
        copy.start()
    _, block, lags = theirs_ref.shape
    chip_block = 2 * block
    per_cycle = CHUNK
    lane, sublane = iota((SUBLANES, LANES), 1), iota((SUBLANES, LANES), 0)
    tiles = lags // LANES
    stores = []
    for cycle in range(count):

        def rows_of(number):
            return jnp.concatenate(
                [
                    ref[source, (first + cycle) * per_cycle : (first + cycle + 1) * per_cycle, :]
                    for ref, first in windows[number]
                    for source in range(ref.shape[0])
                ],
                axis=0,
            )

        columns = [rows_of(number) for number in range(len(windows))]
        own = columns[0]
        at, even, odd = choice
        chosen = jnp.where(lax.rem(chip, 2) == 0, columns[even], columns[odd])
        columns = [
            value
            for number, value in enumerate(columns)
            if number not in (even, odd) and (number or phase == 0)
        ]
        columns.insert(at, chosen)
        whole = jnp.concatenate(columns, axis=1)
        depth, width = whole.shape
        own_rows = own.T
        ones = jnp.ones((PACKED, depth), jnp.bfloat16)
        gram[cycle] = dot(jnp.concatenate([own_rows, ones], axis=0), whole)
        sums = gram[cycle, chip_block : chip_block + SUBLANES, :]
        frame_at = chip * chip_block + phase * lags + iota((SUBLANES, width), 1)
        later[cycle] = jnp.where(frame_at < frame_count, 1.0 / sums, 0.0)
        label = (mod * 2 + core) * group + offset + cycle
        total = counts_ref[pl.ds(label, 1), :]
        for source in range(sent_ref.shape[0]):
            sent = sent_ref[source, sent_ref.shape[1] - CYCLES :, :LANES].astype(jnp.float32)
            total += jnp.sum(
                jnp.where(iota((CYCLES, LANES), 0) == label, sent, 0.0), axis=0, keepdims=True
            )
        own_sums = jnp.sum(own_rows.astype(jnp.float32), axis=1, keepdims=True)
        earlier[cycle] = jnp.broadcast_to(total / own_sums, (chip_block, LANES))
        for target, position in ((theirs_ref, 1 - core), (mine_ref, core)):
            base = pl.multiple_of(position * block, block)
            scales = [
                later[cycle, :, pl.ds(pl.multiple_of(base + tile * LANES, LANES), LANES)]
                for tile in range(tiles + 1)
            ]
            for batch in range(0, block, BATCH):
                results = []
                for first in range(batch, batch + BATCH, SUBLANES):
                    factor = earlier[cycle, pl.ds(base + first, SUBLANES), :]
                    kept = lane + sublane < LANES - first
                    turned = lax.rem(lane + sublane + first, LANES)
                    rolled = []
                    for tile in range(tiles + 1):
                        column = pl.multiple_of(base + tile * LANES, LANES)
                        value = gram[cycle, pl.ds(base + first, SUBLANES), pl.ds(column, LANES)]
                        value = value * factor * scales[tile]
                        rolled.append(
                            jnp.take_along_axis(value, turned, axis=1, mode="promise_in_bounds")
                        )
                    for tile in range(tiles):
                        results.append(jnp.where(kept, rolled[tile], rolled[tile + 1]))
                at = 0
                for first in range(batch, batch + BATCH, SUBLANES):
                    for tile in range(tiles):
                        target[
                            cycle, first : first + SUBLANES, tile * LANES : (tile + 1) * LANES
                        ] = results[at]
                        at += 1
        store = pltpu.make_async_copy(
            mine_ref.at[cycle],
            out_ref.at[core * group + offset + cycle, :, pl.ds(phase * lags, lags)],
            sems.at[cycle],
        )
        store.start()
        stores.append(store)
    for copy in stores + fills:
        copy.wait()


def grams(place, counts, sent, whole, windows, choice, sizes, phase, frame_count, ready):
    group_cycles, cycle_dev, offset, count = sizes
    flat = [piece for pieces in windows for piece, _ in pieces]
    chip_block = flat[0].shape[-1]
    block = chip_block // 2
    depth = sum(piece.shape[0] for piece, _ in windows[0]) * CHUNK
    lags = LAG // 2
    width = lags + chip_block
    kernel = functools.partial(
        gram_kernel,
        layout=[[first for _, first in pieces] for pieces in windows],
        choice=choice,
        frame_count=frame_count,
        group=group_cycles,
        offset=offset,
        count=count,
        phase=phase,
        spots=[spot for _, spot in ready],
        chained=whole is not None,
    )
    operands = [place, counts, sent] + flat + [part for part, _ in ready]
    in_specs = [SMEM_SPEC] + [VMEM_SPEC] * (2 + len(flat)) + [ANY_SPEC] * len(ready)
    aliases = {}
    if whole is not None:
        aliases = {len(operands): 0}
        operands.append(whole)
        in_specs.append(ANY_SPEC)
    return pl.pallas_call(
        kernel,
        out_shape=[
            jax.ShapeDtypeStruct((cycle_dev, block, LAG), jnp.float32),
            jax.ShapeDtypeStruct((count, block, lags), jnp.float32),
        ],
        in_specs=in_specs,
        out_specs=[ANY_SPEC, VMEM_SPEC],
        scratch_shapes=[
            pltpu.VMEM((count, block, lags), jnp.float32),
            pltpu.VMEM((count, chip_block + PACKED, width), jnp.float32),
            pltpu.VMEM((count, SUBLANES, width), jnp.float32),
            pltpu.VMEM((count, chip_block, LANES), jnp.float32),
            pltpu.SemaphoreType.DMA((count,)),
            pltpu.SemaphoreType.DMA((max(1, len(ready)),)),
        ],
        input_output_aliases=aliases,
        compiler_params=params(),
        cost_estimate=estimate(
            2 * count * depth * width * chip_block, 4 * count * chip_block * lags
        ),
    )(*operands)


def fill_copies(core, part_refs, spots, out_ref, sems):
    copies = []
    for number, (part_ref, (group, offset, lag)) in enumerate(zip(part_refs, spots)):
        cycles, _, lags = part_ref.shape
        first = (1 - core) * group + offset
        copies.append(
            pltpu.make_async_copy(
                part_ref,
                out_ref.at[pl.ds(first, cycles), :, pl.ds(lag, lags)],
                sems.at[number],
            )
        )
    return copies


def fill_kernel(place_ref, *rest, spots):
    part_refs, out_ref, sems = rest[: len(spots)], rest[-2], rest[-1]
    copies = fill_copies(place_ref[0], part_refs, spots, out_ref, sems)
    for copy in copies:
        copy.start()
    for copy in copies:
        copy.wait()


def fill(place, whole, ready):
    parts, spots = zip(*ready)
    return pl.pallas_call(
        functools.partial(fill_kernel, spots=spots),
        out_shape=jax.ShapeDtypeStruct(whole.shape, whole.dtype),
        in_specs=[SMEM_SPEC] + [ANY_SPEC] * (len(parts) + 1),
        out_specs=ANY_SPEC,
        scratch_shapes=[pltpu.SemaphoreType.DMA((len(parts),))],
        input_output_aliases={1 + len(parts): 0},
        compiler_params=params(),
        cost_estimate=estimate(0, 8 * sum(part.size for part in parts)),
    )(place, *parts, whole)


def shifted(value, pairs_down):
    step = 2 * pairs_down
    count = lax.axis_size("frame")
    return lax.ppermute(value, "frame", [(source, source - step) for source in range(step, count)])


def other_pair(value, parity=None):
    count = lax.axis_size("frame")
    sources = [at for at in range(count) if parity is None or at // 2 % 2 == parity]
    return lax.ppermute(value, "frame", [(source, source ^ 2) for source in sources])


def other_core(value):
    count = lax.axis_size("frame")
    return lax.ppermute(value, "frame", [(source, source ^ 1) for source in range(count)])


def along_mod(value, step, odd_pairs=False):
    frames, mods = lax.axis_size("frame"), lax.axis_size("mod")
    pairs = [
        (frame * mods + mod, (frame - 2 * odd_pairs) * mods + (mod + step) % mods)
        for frame in range(frames)
        for mod in range(mods)
        if not odd_pairs or frame // 2 % 2
    ]
    return lax.ppermute(value, ("frame", "mod"), pairs)


def shards(frames, cycle_label, good_pixel):
    mods = lax.axis_size("mod")
    cycle_dev = CYCLES // mods
    group_cycles = cycle_dev // 2
    mod, frame = lax.axis_index("mod"), lax.axis_index("frame")
    core, chip = frame % 2, frame // 2
    block, pix_count = frames.shape
    frame_count = block * lax.axis_size("frame")
    assert LAG == 8 * block and block == LANES and pix_count == CYCLES * CHUNK
    place = jnp.stack([core, chip, mod]).astype(jnp.int32)
    half = group_cycles // 2
    parts = [half, group_cycles - half] if half else [group_cycles]
    offsets = [sum(parts[:number]) for number in range(len(parts))]

    halves = len(parts)
    own_units = halves if OWN_SPLIT else 1
    other = other_core(frames)
    used = jnp.where(good_pixel > 0, cycle_label, CYCLES)
    key, counts, own_frames = rank_pixels(used, frames)
    done = {}

    def tied(value, name):
        ties = [get(tie) for tie in TIES.get(name, ()) if known(tie)]
        ties = [tie[0] if isinstance(tie, (list, tuple)) else tie for tie in ties]
        return lax.optimization_barrier((value, *ties))[0] if ties else value

    def known(name):
        limits = dict(g=halves, s=halves, y=halves, k=mods, o=2)
        return all(int(at) < limits.get(name[0], own_units + halves) for at in name[-1])

    def get(name):
        if name not in done:
            done[name] = make(name[0], name, *(int(at) for at in name[1:]))
        return done[name]

    def make(kind, name, first, second=0):
        if kind == "k":
            joined = [own_frames, other] if first == 0 else [get("k0")[-1]]
            split = first > 0 or own_units > 1
            return order_pixels(place, tied(key, name), counts, joined, first, mods, parts, split)
        if kind == "y":
            return jnp.stack(
                [along_mod(tied(get(f"k{step}")[1 + first], name), step) for step in range(1, mods)]
            )
        if kind == "u":
            if first >= own_units:
                return get(f"y{first - own_units}")
            return get("k0")[1 + first if own_units > 1 else 0][None]
        if kind == "z":
            return shifted(tied(get(f"u{first}"), name), 2)
        if kind == "w":
            return shifted(tied(get(f"z{first}"), name), 2)
        if kind == "x":
            return other_pair(tied(get(f"z{first}"), name))
        if kind == "v":
            return other_pair(tied(get(f"w{first}"), name), 0)
        if kind == "o":
            if first == 0:
                return other_pair(tied(get("k0")[0], name), 1)[None]
            return jnp.stack(
                [along_mod(tied(get(f"k{step}")[0], name), step, True) for step in range(1, mods)]
            )
        if kind == "s":
            return other_core(get(f"g{first}{second}")[1])
        assert kind == "g"
        phase, part = first, second

        def both(letter):
            early = (get(f"{letter}{part}"), 0) if own_units > 1 else (get(f"{letter}0"), offsets[part])
            return [early, (get(f"{letter}{own_units + part}"), 0)]

        if phase == 0:
            neighbour = [(get(f"o{at}"), offsets[part]) for at in range(2)]
            windows, choice = [both("u"), both("z"), neighbour, both("x")], (1, 2, 3)
        else:
            windows = [both(letter) for letter in "uzwxv"]
            choice = (1, 3, 4)
        before = phase * halves + part - 1
        whole = get(f"g{before // halves}{before % halves}")[0] if before >= 0 else None
        filled = [spot(0, at) for at in range(halves)] if phase and not part else []
        sizes = (group_cycles, cycle_dev, offsets[part], parts[part])
        return grams(
            place, tied(counts, name), get(f"u{own_units}"), whole, windows, choice, sizes, phase, frame_count, filled
        )

    def spot(phase, part):
        return get(f"s{phase}{part}"), (group_cycles, offsets[part], phase * (LAG // 2))

    whole = get(f"g1{halves - 1}")[0]
    return fill(place, whole, [spot(1, part) for part in range(halves)])


def solution(mesh):
    placed = (P("frame", "mod"), P("mod"), P("mod"))
    return jax.shard_map(
        shards, mesh=mesh, in_specs=placed, out_specs=P("mod", "frame", None), check_vma=False
    )
```

```python
import functools

import jax
import jax.numpy as jnp
from jax import lax
from jax.experimental import pallas as pl
from jax.experimental.pallas import tpu as pltpu
from jax.sharding import PartitionSpec as P

CYCLES = 16
LAG = 1024
LANES = 128
SUBLANES = 8
PACKED = 16
BATCH = 64
CHUNK = 256
VMEM_LIMIT = 24 * 1024 * 1024

ORDER = (
    ("start", "o0", "z0", "y0"),
    ("wait", "k1"),
    ("start", "z1"),
    ("wait", "z0"),
    ("pause", 1000000000),
    ("start", "w0", "x0"),
    ("wait", "y0"),
    ("start", "z2"),
    ("wait", "o0"),
    ("start", "x1", "w1"),
    ("wait", "w0"),
    ("start", "v0"),
    ("wait", "z1", "x0"),
    ("start", "y1", "x2", "w2"),
    ("wait", "x1"),
    ("start", "v1", "o1"),
    ("wait", "z2", "y1", "v0", "w1"),
    ("start", "z3"),
    ("pause", 100000000),
    ("pause", 300000000),
    ("pause", 0),
    ("wait", "w0", "x2"),
    ("pause", 100000000),
    ("start", "v2"),
    ("wait", "w2", "v1"),
    ("start", "w3", "x3"),
    ("pause", 300000000),
    ("wait", "o1", "v2", "g00"),
    ("start", "v3"),
    ("wait", "x3", "g01", "g11", "v3", "g10"),
)
OWN_SPLIT = True

SMEM_SPEC = pl.BlockSpec(memory_space=pltpu.SMEM)
VMEM_SPEC = pl.BlockSpec(memory_space=pltpu.VMEM)
HBM_SPEC = pl.BlockSpec(memory_space=pltpu.HBM)
ANY_SPEC = pl.BlockSpec(memory_space=pl.ANY)

dot = functools.partial(jnp.dot, preferred_element_type=jnp.float32)


def params():
    return pltpu.CompilerParams(vmem_limit_bytes=VMEM_LIMIT)


def estimate(flops, moved):
    return pl.CostEstimate(flops=flops, bytes_accessed=moved, transcendentals=0)


def ones_where(condition):
    return jnp.where(condition, 1.0, 0.0).astype(jnp.bfloat16)


def iota(shape, dimension):
    return lax.broadcasted_iota(jnp.int32, shape, dimension)


def rank_kernel(label_ref, frames_hbm, key_ref, counts_ref, frames_ref, sem):
    copy = pltpu.make_async_copy(frames_hbm, frames_ref, sem)
    copy.start()
    chunks = label_ref.shape[0] // CHUNK
    rows = chunks * CYCLES
    up, across = iota((rows, rows), 0), iota((rows, rows), 1)
    same = lax.rem(up, CYCLES) == lax.rem(across, CYCLES)
    chunk_before = ones_where(same & (across < up))
    before = ones_where(iota((CHUNK, CHUNK), 0) < iota((CHUNK, CHUNK), 1))
    of_cycle = ones_where(iota((CYCLES, rows), 0) == lax.rem(iota((CYCLES, rows), 1), CYCLES))
    cycle_at = iota((CYCLES, CHUNK), 0)
    labels = [label_ref[pl.ds(at * CHUNK, CHUNK)].reshape(1, CHUNK) for at in range(chunks)]
    used = jnp.concatenate([jnp.where(one == cycle_at, 1.0, 0.0) for one in labels], axis=0)
    member = used.astype(jnp.bfloat16)
    earlier = dot(chunk_before, member).astype(jnp.bfloat16)
    rank = dot(member, before) + dot(earlier, jnp.ones((CHUNK, CHUNK), jnp.bfloat16))
    key_ref[...] = jnp.where(used > 0.0, rank, -1.0)
    per_lane = dot(of_cycle, member).astype(jnp.bfloat16)
    counts_ref[...] = dot(per_lane, jnp.ones((CHUNK, LANES), jnp.bfloat16))
    copy.wait()


def rank_pixels(label, frames):
    rows = label.shape[0] // CHUNK * CYCLES
    return pl.pallas_call(
        rank_kernel,
        out_shape=[
            jax.ShapeDtypeStruct((rows, CHUNK), jnp.float32),
            jax.ShapeDtypeStruct((CYCLES, LANES), jnp.float32),
            jax.ShapeDtypeStruct(frames.shape, frames.dtype),
        ],
        in_specs=[VMEM_SPEC, HBM_SPEC],
        out_specs=[VMEM_SPEC] * 3,
        scratch_shapes=[pltpu.SemaphoreType.DMA],
        compiler_params=params(),
        cost_estimate=estimate(6 * rows * CHUNK * CHUNK, 8 * label.shape[0]),
    )(label, pltpu.with_memory_space_constraint(frames, pltpu.HBM))


def order_kernel(place_ref, key_ref, counts_ref, *rest, step, mods, parts, joined):
    rest = list(rest)
    core, mod = place_ref[0], place_ref[2]
    if joined:
        frames_ref = rest.pop(0)
    else:
        own_ref, other_ref, frames_ref = rest.pop(0), rest.pop(0), rest.pop()
        block = own_ref.shape[0]
        frames_ref[pl.ds(pl.multiple_of(core * block, block), block), :] = own_ref[...]
        frames_ref[pl.ds(pl.multiple_of((1 - core) * block, block), block), :] = other_ref[...]
    frames = frames_ref[...]
    all_ref, part_refs = rest[0], rest[1:]
    chunks = key_ref.shape[0] // CYCLES
    per_cycle = frames.shape[1] // CYCLES
    first_cycle = (lax.rem(mod + step, mods) * 2 + core) * sum(parts)
    if step:
        row = parts[0] * per_cycle
        sent = jnp.concatenate([counts_ref[...]] * (frames.shape[0] // LANES), axis=1)
        part_refs[0][row : row + CYCLES, :] = sent.astype(jnp.bfloat16)
    slots = [
        (iota((PACKED, CHUNK), 0) + first).astype(jnp.float32).astype(jnp.bfloat16)
        for first in range(0, per_cycle, PACKED)
    ]
    one = jnp.ones((PACKED, CHUNK), jnp.bfloat16)
    zero = jnp.zeros((PACKED, CHUNK), jnp.bfloat16)
    spots = [(number, at) for number, part in enumerate(parts) for at in range(part)]
    for cycle, (number, at) in enumerate(spots):
        tiles = []
        for chunk in range(chunks):
            key = key_ref[pl.ds(chunk * CYCLES + first_cycle + cycle, 1), :]
            key = jnp.broadcast_to(key, (PACKED, CHUNK)).astype(jnp.bfloat16)
            tiles.append(
                jnp.concatenate([jnp.where(key == slot, one, zero) for slot in slots], axis=0)
            )
        picked = lax.dot_general(
            jnp.concatenate(tiles, axis=1),
            frames,
            (((1,), (1,)), ((), ())),
            preferred_element_type=jnp.float32,
        ).astype(jnp.bfloat16)
        all_ref[cycle * per_cycle : (cycle + 1) * per_cycle, :] = picked
        if part_refs:
            part_refs[number][at * per_cycle : (at + 1) * per_cycle, :] = picked


def order_pixels(place, key, counts, frames, step, mods, parts, split):
    joined = len(frames) == 1
    chip_block = frames[0].shape[0] * (1 if joined else 2)
    pix_count = frames[0].shape[1]
    per_cycle = pix_count // CYCLES
    heights = [part * per_cycle for part in [sum(parts)] + (list(parts) if split else [])]
    if step:
        heights[1] += CYCLES
    out_shape = [jax.ShapeDtypeStruct((height, chip_block), jnp.bfloat16) for height in heights]
    if not joined:
        out_shape.append(jax.ShapeDtypeStruct((chip_block, pix_count), jnp.bfloat16))
    return pl.pallas_call(
        functools.partial(order_kernel, step=step, mods=mods, parts=parts, joined=joined),
        out_shape=out_shape,
        in_specs=[SMEM_SPEC] + [VMEM_SPEC] * (2 + len(frames)),
        out_specs=[VMEM_SPEC] * len(out_shape),
        compiler_params=params(),
        cost_estimate=estimate(
            2 * sum(parts) * per_cycle * pix_count * chip_block, 2 * pix_count * chip_block
        ),
    )(place, key, counts, *frames)


def gram_kernel(place_ref, counts_ref, sent_ref, *rest, layout, choice, frame_count, group, offset, count, phase, spots, chained):
    rest = list(rest)
    windows = [[(rest.pop(0), first) for first in pieces] for pieces in layout]
    ready_refs = [rest.pop(0) for _ in spots]
    if chained:
        rest.pop(0)
    out_ref, theirs_ref, mine_ref, gram, later, earlier, sems, fill_sems = rest
    core, chip, mod = place_ref[0], place_ref[1], place_ref[2]
    fills = fill_copies(core, ready_refs, spots, out_ref, fill_sems)
    for copy in fills:
        copy.start()
    _, block, lags = theirs_ref.shape
    chip_block = 2 * block
    per_cycle = CHUNK
    lane, sublane = iota((SUBLANES, LANES), 1), iota((SUBLANES, LANES), 0)
    tiles = lags // LANES
    stores = []
    for cycle in range(count):

        def rows_of(number):
            return jnp.concatenate(
                [
                    ref[source, (first + cycle) * per_cycle : (first + cycle + 1) * per_cycle, :]
                    for ref, first in windows[number]
                    for source in range(ref.shape[0])
                ],
                axis=0,
            )

        columns = [rows_of(number) for number in range(len(windows))]
        own = columns[0]
        at, even, odd = choice
        chosen = jnp.where(lax.rem(chip, 2) == 0, columns[even], columns[odd])
        columns = [
            value
            for number, value in enumerate(columns)
            if number not in (even, odd) and (number or phase == 0)
        ]
        columns.insert(at, chosen)
        whole = jnp.concatenate(columns, axis=1)
        depth, width = whole.shape
        own_rows = own.T
        ones = jnp.ones((PACKED, depth), jnp.bfloat16)
        gram[cycle] = dot(jnp.concatenate([own_rows, ones], axis=0), whole)
        sums = gram[cycle, chip_block : chip_block + SUBLANES, :]
        frame_at = chip * chip_block + phase * lags + iota((SUBLANES, width), 1)
        later[cycle] = jnp.where(frame_at < frame_count, 1.0 / sums, 0.0)
        label = (mod * 2 + core) * group + offset + cycle
        total = counts_ref[pl.ds(label, 1), :]
        for source in range(sent_ref.shape[0]):
            sent = sent_ref[source, sent_ref.shape[1] - CYCLES :, :LANES].astype(jnp.float32)
            total += jnp.sum(
                jnp.where(iota((CYCLES, LANES), 0) == label, sent, 0.0), axis=0, keepdims=True
            )
        own_sums = jnp.sum(own_rows.astype(jnp.float32), axis=1, keepdims=True)
        earlier[cycle] = jnp.broadcast_to(total / own_sums, (chip_block, LANES))
        for target, position in ((theirs_ref, 1 - core), (mine_ref, core)):
            base = pl.multiple_of(position * block, block)
            scales = [
                later[cycle, :, pl.ds(pl.multiple_of(base + tile * LANES, LANES), LANES)]
                for tile in range(tiles + 1)
            ]
            for batch in range(0, block, BATCH):
                results = []
                for first in range(batch, batch + BATCH, SUBLANES):
                    factor = earlier[cycle, pl.ds(base + first, SUBLANES), :]
                    kept = lane + sublane < LANES - first
                    turned = lax.rem(lane + sublane + first, LANES)
                    rolled = []
                    for tile in range(tiles + 1):
                        column = pl.multiple_of(base + tile * LANES, LANES)
                        value = gram[cycle, pl.ds(base + first, SUBLANES), pl.ds(column, LANES)]
                        value = value * factor * scales[tile]
                        rolled.append(
                            jnp.take_along_axis(value, turned, axis=1, mode="promise_in_bounds")
                        )
                    for tile in range(tiles):
                        results.append(jnp.where(kept, rolled[tile], rolled[tile + 1]))
                at = 0
                for first in range(batch, batch + BATCH, SUBLANES):
                    for tile in range(tiles):
                        target[
                            cycle, first : first + SUBLANES, tile * LANES : (tile + 1) * LANES
                        ] = results[at]
                        at += 1
        store = pltpu.make_async_copy(
            mine_ref.at[cycle],
            out_ref.at[core * group + offset + cycle, :, pl.ds(phase * lags, lags)],
            sems.at[cycle],
        )
        store.start()
        stores.append(store)
    for copy in stores + fills:
        copy.wait()


def grams(place, counts, sent, whole, windows, choice, sizes, phase, frame_count, ready):
    group_cycles, cycle_dev, offset, count = sizes
    flat = [piece for pieces in windows for piece, _ in pieces]
    chip_block = flat[0].shape[-1]
    block = chip_block // 2
    depth = sum(piece.shape[0] for piece, _ in windows[0]) * CHUNK
    lags = LAG // 2
    width = lags + chip_block
    kernel = functools.partial(
        gram_kernel,
        layout=[[first for _, first in pieces] for pieces in windows],
        choice=choice,
        frame_count=frame_count,
        group=group_cycles,
        offset=offset,
        count=count,
        phase=phase,
        spots=[spot for _, spot in ready],
        chained=whole is not None,
    )
    operands = [place, counts, sent] + flat + [part for part, _ in ready]
    in_specs = [SMEM_SPEC] + [VMEM_SPEC] * (2 + len(flat)) + [ANY_SPEC] * len(ready)
    aliases = {}
    if whole is not None:
        aliases = {len(operands): 0}
        operands.append(whole)
        in_specs.append(ANY_SPEC)
    return pl.pallas_call(
        kernel,
        out_shape=[
            jax.ShapeDtypeStruct((cycle_dev, block, LAG), jnp.float32),
            jax.ShapeDtypeStruct((count, block, lags), jnp.float32),
        ],
        in_specs=in_specs,
        out_specs=[ANY_SPEC, VMEM_SPEC],
        scratch_shapes=[
            pltpu.VMEM((count, block, lags), jnp.float32),
            pltpu.VMEM((count, chip_block + PACKED, width), jnp.float32),
            pltpu.VMEM((count, SUBLANES, width), jnp.float32),
            pltpu.VMEM((count, chip_block, LANES), jnp.float32),
            pltpu.SemaphoreType.DMA((count,)),
            pltpu.SemaphoreType.DMA((max(1, len(ready)),)),
        ],
        input_output_aliases=aliases,
        compiler_params=params(),
        cost_estimate=estimate(
            2 * count * depth * width * chip_block, 4 * count * chip_block * lags
        ),
    )(*operands)


def fill_copies(core, part_refs, spots, out_ref, sems):
    copies = []
    for number, (part_ref, (group, offset, lag)) in enumerate(zip(part_refs, spots)):
        cycles, _, lags = part_ref.shape
        first = (1 - core) * group + offset
        copies.append(
            pltpu.make_async_copy(
                part_ref,
                out_ref.at[pl.ds(first, cycles), :, pl.ds(lag, lags)],
                sems.at[number],
            )
        )
    return copies


def fill_kernel(place_ref, *rest, spots):
    part_refs, out_ref, sems = rest[: len(spots)], rest[-2], rest[-1]
    copies = fill_copies(place_ref[0], part_refs, spots, out_ref, sems)
    for copy in copies:
        copy.start()
    for copy in copies:
        copy.wait()


def fill(place, token, whole, ready):
    parts, spots = zip(*ready)
    return pl.pallas_call(
        functools.partial(fill_kernel, spots=spots),
        out_shape=jax.ShapeDtypeStruct(whole.shape, whole.dtype),
        in_specs=[SMEM_SPEC] + [ANY_SPEC] * (len(parts) + 2),
        out_specs=ANY_SPEC,
        scratch_shapes=[pltpu.SemaphoreType.DMA((len(parts),))],
        input_output_aliases={2 + len(parts): 0},
        compiler_params=params(),
        cost_estimate=estimate(0, 8 * sum(part.size for part in parts)),
    )(place, *parts, token, whole)


def pause_kernel(value_ref, out_ref):
    out_ref[...] = value_ref[...]


def pause(value, weight):
    return pl.pallas_call(
        pause_kernel,
        out_shape=jax.ShapeDtypeStruct(value.shape, value.dtype),
        in_specs=[VMEM_SPEC],
        out_specs=VMEM_SPEC,
        cost_estimate=estimate(weight, 0),
    )(value)


def shifted(value, pairs_down):
    step = 2 * pairs_down
    count = lax.axis_size("frame")
    return lax.ppermute(value, "frame", [(source, source - step) for source in range(step, count)])


def other_pair(value, parity=None):
    count = lax.axis_size("frame")
    sources = [at for at in range(count) if parity is None or at // 2 % 2 == parity]
    return lax.ppermute(value, "frame", [(source, source ^ 2) for source in sources])


def other_core(value):
    count = lax.axis_size("frame")
    return lax.ppermute(value, "frame", [(source, source ^ 1) for source in range(count)])


def along_mod(value, step, odd_pairs=False):
    frames, mods = lax.axis_size("frame"), lax.axis_size("mod")
    pairs = [
        (frame * mods + mod, (frame - 2 * odd_pairs) * mods + (mod + step) % mods)
        for frame in range(frames)
        for mod in range(mods)
        if not odd_pairs or frame // 2 % 2
    ]
    return lax.ppermute(value, ("frame", "mod"), pairs)


def shards(frames, cycle_label, good_pixel):
    mods = lax.axis_size("mod")
    cycle_dev = CYCLES // mods
    group_cycles = cycle_dev // 2
    mod, frame = lax.axis_index("mod"), lax.axis_index("frame")
    core, chip = frame % 2, frame // 2
    block, pix_count = frames.shape
    frame_count = block * lax.axis_size("frame")
    assert LAG == 8 * block and block == LANES and pix_count == CYCLES * CHUNK
    place = jnp.stack([core, chip, mod]).astype(jnp.int32)
    half = group_cycles // 2
    parts = [half, group_cycles - half] if half else [group_cycles]
    offsets = [sum(parts[:number]) for number in range(len(parts))]

    halves = len(parts)
    own_units = halves if OWN_SPLIT else 1
    other = other_core(frames)
    used = jnp.where(good_pixel > 0, cycle_label, CYCLES)
    key, counts, own_frames = rank_pixels(used, frames)
    done = {}

    token = counts

    def tied(value, name):
        nonlocal token
        value, token = lax.optimization_barrier((value, token))
        return value

    def known(name):
        limits = dict(g=halves, s=halves, y=halves, k=mods, o=2)
        return all(int(at) < limits.get(name[0], own_units + halves) for at in name[-1])

    def get(name):
        if name not in done:
            done[name] = make(name[0], name, *(int(at) for at in name[1:]))
        return done[name]

    def make(kind, name, first, second=0):
        if kind == "k":
            joined = [own_frames, other] if first == 0 else [get("k0")[-1]]
            split = first > 0 or own_units > 1
            return order_pixels(place, tied(key, name), counts, joined, first, mods, parts, split)
        if kind == "y":
            return jnp.stack(
                [along_mod(tied(get(f"k{step}")[1 + first], name), step) for step in range(1, mods)]
            )
        if kind == "u":
            if first >= own_units:
                return get(f"y{first - own_units}")
            return get("k0")[1 + first if own_units > 1 else 0][None]
        if kind == "z":
            return shifted(tied(get(f"u{first}"), name), 2)
        if kind == "w":
            return shifted(tied(get(f"z{first}"), name), 2)
        if kind == "x":
            return other_pair(tied(get(f"z{first}"), name))
        if kind == "v":
            return other_pair(tied(get(f"w{first}"), name), 0)
        if kind == "o":
            if first == 0:
                return other_pair(tied(get("k0")[0], name), 1)[None]
            return jnp.stack(
                [along_mod(tied(get(f"k{step}")[0], name), step, True) for step in range(1, mods)]
            )
        if kind == "s":
            return other_core(get(f"g{first}{second}")[1])
        assert kind == "g"
        phase, part = first, second

        def both(letter):
            early = (get(f"{letter}{part}"), 0) if own_units > 1 else (get(f"{letter}0"), offsets[part])
            return [early, (get(f"{letter}{own_units + part}"), 0)]

        if phase == 0:
            neighbour = [(get(f"o{at}"), offsets[part]) for at in range(2)]
            windows, choice = [both("u"), both("z"), neighbour, both("x")], (1, 2, 3)
        else:
            windows = [both(letter) for letter in "uzwxv"]
            choice = (1, 3, 4)
        before = phase * halves + part - 1
        whole = get(f"g{before // halves}{before % halves}")[0] if before >= 0 else None
        filled = [spot(0, at) for at in range(halves)] if phase and not part else []
        sizes = (group_cycles, cycle_dev, offsets[part], parts[part])
        return grams(
            place, tied(counts, name), get(f"u{own_units}"), whole, windows, choice, sizes, phase, frame_count, filled
        )

    def spot(phase, part):
        return get(f"s{phase}{part}"), (group_cycles, offsets[part], phase * (LAG // 2))

    for step, *names in ORDER:
        if step == "pause":
            token = pause(token, *names)
            continue
        for name in filter(known, names):
            value = get(name)
            if step == "wait":
                if isinstance(value, (list, tuple)):
                    head, token = lax.optimization_barrier((value[0], token))
                    done[name] = [head, *value[1:]]
                else:
                    done[name], token = lax.optimization_barrier((value, token))
    whole = get(f"g1{halves - 1}")[0]
    return fill(place, token, whole, [spot(1, part) for part in range(halves)])


def solution(mesh):
    placed = (P("frame", "mod"), P("mod"), P("mod"))
    return jax.shard_map(
        shards, mesh=mesh, in_specs=placed, out_specs=P("mod", "frame", None), check_vma=False
    )
```

```python
import functools

import jax
import jax.numpy as jnp
from jax import lax
from jax.experimental import pallas as pl
from jax.experimental.pallas import tpu as pltpu
from jax.sharding import PartitionSpec as P

CYCLES = 16
LAG = 1024
LANES = 128
SUBLANES = 8
PACKED = 16
BATCH = 64
CHUNK = 256
VMEM_LIMIT = 24 * 1024 * 1024

ORDER = (
    ("start", "o0", "z0", "y0"),
    ("wait", "k1"),
    ("start", "z1"),
    ("wait", "z0"),
    ("pause", 1000000000),
    ("start", "w0", "x0"),
    ("wait", "y0"),
    ("start", "z2"),
    ("wait", "o0"),
    ("start", "x1", "w1"),
    ("wait", "w0"),
    ("start", "v0"),
    ("wait", "z1", "x0"),
    ("start", "y1", "x2", "w2"),
    ("wait", "x1"),
    ("start", "v1", "o1"),
    ("wait", "z2", "y1", "v0", "w1"),
    ("start", "z3"),
    ("pause", 100000000),
    ("pause", 300000000),
    ("pause", 0),
    ("wait", "w0", "x2"),
    ("pause", 100000000),
    ("start", "v2"),
    ("wait", "w2", "v1"),
    ("start", "w3", "x3"),
    ("pause", 300000000),
    ("wait", "o1", "v2", "g00"),
    ("start", "v3"),
    ("wait", "x3", "g01", "g11", "v3", "g10"),
)
OWN_SPLIT = True

SMEM_SPEC = pl.BlockSpec(memory_space=pltpu.SMEM)
VMEM_SPEC = pl.BlockSpec(memory_space=pltpu.VMEM)
HBM_SPEC = pl.BlockSpec(memory_space=pltpu.HBM)
ANY_SPEC = pl.BlockSpec(memory_space=pl.ANY)

dot = functools.partial(jnp.dot, preferred_element_type=jnp.float32)


def params():
    return pltpu.CompilerParams(vmem_limit_bytes=VMEM_LIMIT)


def estimate(flops, moved):
    return pl.CostEstimate(flops=flops, bytes_accessed=moved, transcendentals=0)


def ones_where(condition):
    return jnp.where(condition, 1.0, 0.0).astype(jnp.bfloat16)


def iota(shape, dimension):
    return lax.broadcasted_iota(jnp.int32, shape, dimension)


def rank_kernel(label_ref, frames_hbm, key_ref, counts_ref, frames_ref, sem):
    copy = pltpu.make_async_copy(frames_hbm, frames_ref, sem)
    copy.start()
    chunks = label_ref.shape[0] // CHUNK
    rows = chunks * CYCLES
    up, across = iota((rows, rows), 0), iota((rows, rows), 1)
    same = lax.rem(up, CYCLES) == lax.rem(across, CYCLES)
    chunk_before = ones_where(same & (across < up))
    before = ones_where(iota((CHUNK, CHUNK), 0) < iota((CHUNK, CHUNK), 1))
    of_cycle = ones_where(iota((CYCLES, rows), 0) == lax.rem(iota((CYCLES, rows), 1), CYCLES))
    cycle_at = iota((CYCLES, CHUNK), 0)
    labels = [label_ref[pl.ds(at * CHUNK, CHUNK)].reshape(1, CHUNK) for at in range(chunks)]
    used = jnp.concatenate([jnp.where(one == cycle_at, 1.0, 0.0) for one in labels], axis=0)
    member = used.astype(jnp.bfloat16)
    earlier = dot(chunk_before, member).astype(jnp.bfloat16)
    rank = dot(member, before) + dot(earlier, jnp.ones((CHUNK, CHUNK), jnp.bfloat16))
    key_ref[...] = jnp.where(used > 0.0, rank, -1.0)
    per_lane = dot(of_cycle, member).astype(jnp.bfloat16)
    counts_ref[...] = dot(per_lane, jnp.ones((CHUNK, LANES), jnp.bfloat16))
    copy.wait()


def rank_pixels(label, frames):
    rows = label.shape[0] // CHUNK * CYCLES
    return pl.pallas_call(
        rank_kernel,
        out_shape=[
            jax.ShapeDtypeStruct((rows, CHUNK), jnp.float32),
            jax.ShapeDtypeStruct((CYCLES, LANES), jnp.float32),
            jax.ShapeDtypeStruct(frames.shape, frames.dtype),
        ],
        in_specs=[VMEM_SPEC, HBM_SPEC],
        out_specs=[VMEM_SPEC] * 3,
        scratch_shapes=[pltpu.SemaphoreType.DMA],
        compiler_params=params(),
        cost_estimate=estimate(6 * rows * CHUNK * CHUNK, 8 * label.shape[0]),
    )(label, pltpu.with_memory_space_constraint(frames, pltpu.HBM))


def order_kernel(place_ref, key_ref, counts_ref, *rest, step, mods, parts, joined):
    rest = list(rest)
    core, mod = place_ref[0], place_ref[2]
    if joined:
        frames_ref = rest.pop(0)
    else:
        own_ref, other_ref, frames_ref = rest.pop(0), rest.pop(0), rest.pop()
        block = own_ref.shape[0]
        frames_ref[pl.ds(pl.multiple_of(core * block, block), block), :] = own_ref[...]
        frames_ref[pl.ds(pl.multiple_of((1 - core) * block, block), block), :] = other_ref[...]
    frames = frames_ref[...]
    all_ref, part_refs = rest[0], rest[1:]
    chunks = key_ref.shape[0] // CYCLES
    per_cycle = frames.shape[1] // CYCLES
    first_cycle = (lax.rem(mod + step, mods) * 2 + core) * sum(parts)
    if step:
        row = parts[0] * per_cycle
        sent = jnp.concatenate([counts_ref[...]] * (frames.shape[0] // LANES), axis=1)
        part_refs[0][row : row + CYCLES, :] = sent.astype(jnp.bfloat16)
    slots = [
        (iota((PACKED, CHUNK), 0) + first).astype(jnp.float32).astype(jnp.bfloat16)
        for first in range(0, per_cycle, PACKED)
    ]
    one = jnp.ones((PACKED, CHUNK), jnp.bfloat16)
    zero = jnp.zeros((PACKED, CHUNK), jnp.bfloat16)
    spots = [(number, at) for number, part in enumerate(parts) for at in range(part)]
    for cycle, (number, at) in enumerate(spots):
        tiles = []
        for chunk in range(chunks):
            key = key_ref[pl.ds(chunk * CYCLES + first_cycle + cycle, 1), :]
            key = jnp.broadcast_to(key, (PACKED, CHUNK)).astype(jnp.bfloat16)
            tiles.append(
                jnp.concatenate([jnp.where(key == slot, one, zero) for slot in slots], axis=0)
            )
        picked = lax.dot_general(
            jnp.concatenate(tiles, axis=1),
            frames,
            (((1,), (1,)), ((), ())),
            preferred_element_type=jnp.float32,
        ).astype(jnp.bfloat16)
        all_ref[cycle * per_cycle : (cycle + 1) * per_cycle, :] = picked
        if part_refs:
            part_refs[number][at * per_cycle : (at + 1) * per_cycle, :] = picked


def order_pixels(place, key, counts, frames, step, mods, parts, split):
    joined = len(frames) == 1
    chip_block = frames[0].shape[0] * (1 if joined else 2)
    pix_count = frames[0].shape[1]
    per_cycle = pix_count // CYCLES
    heights = [part * per_cycle for part in [sum(parts)] + (list(parts) if split else [])]
    if step:
        heights[1] += CYCLES
    out_shape = [jax.ShapeDtypeStruct((height, chip_block), jnp.bfloat16) for height in heights]
    if not joined:
        out_shape.append(jax.ShapeDtypeStruct((chip_block, pix_count), jnp.bfloat16))
    return pl.pallas_call(
        functools.partial(order_kernel, step=step, mods=mods, parts=parts, joined=joined),
        out_shape=out_shape,
        in_specs=[SMEM_SPEC] + [VMEM_SPEC] * (2 + len(frames)),
        out_specs=[VMEM_SPEC] * len(out_shape),
        compiler_params=params(),
        cost_estimate=estimate(
            2 * sum(parts) * per_cycle * pix_count * chip_block, 2 * pix_count * chip_block
        ),
    )(place, key, counts, *frames)


def gram_kernel(place_ref, counts_ref, sent_ref, *rest, layout, choice, frame_count, group, offset, count, phase, spots, chained):
    rest = list(rest)
    windows = [[(rest.pop(0), first) for first in pieces] for pieces in layout]
    ready_refs = [rest.pop(0) for _ in spots]
    if chained:
        rest.pop(0)
    out_ref, theirs_ref, mine_ref, gram, later, earlier, sems, fill_sems = rest
    core, chip, mod = place_ref[0], place_ref[1], place_ref[2]
    fills = fill_copies(core, ready_refs, spots, out_ref, fill_sems)
    for copy in fills:
        copy.start()
    _, block, lags = theirs_ref.shape
    chip_block = 2 * block
    per_cycle = CHUNK
    lane, sublane = iota((SUBLANES, LANES), 1), iota((SUBLANES, LANES), 0)
    tiles = lags // LANES
    stores = []
    for cycle in range(count):

        def rows_of(number):
            return jnp.concatenate(
                [
                    ref[source, (first + cycle) * per_cycle : (first + cycle + 1) * per_cycle, :]
                    for ref, first in windows[number]
                    for source in range(ref.shape[0])
                ],
                axis=0,
            )

        columns = [rows_of(number) for number in range(len(windows))]
        own = columns[0]
        at, even, odd = choice
        chosen = jnp.where(lax.rem(chip, 2) == 0, columns[even], columns[odd])
        columns = [
            value
            for number, value in enumerate(columns)
            if number not in (even, odd) and (number or phase == 0)
        ]
        columns.insert(at, chosen)
        whole = jnp.concatenate(columns, axis=1)
        depth, width = whole.shape
        own_rows = own.T
        ones = jnp.ones((PACKED, depth), jnp.bfloat16)
        gram[cycle] = dot(jnp.concatenate([own_rows, ones], axis=0), whole)
        sums = gram[cycle, chip_block : chip_block + SUBLANES, :]
        frame_at = chip * chip_block + phase * lags + iota((SUBLANES, width), 1)
        later[cycle] = jnp.where(frame_at < frame_count, 1.0 / sums, 0.0)
        label = (mod * 2 + core) * group + offset + cycle
        total = counts_ref[pl.ds(label, 1), :]
        for source in range(sent_ref.shape[0]):
            sent = sent_ref[source, sent_ref.shape[1] - CYCLES :, :LANES].astype(jnp.float32)
            total += jnp.sum(
                jnp.where(iota((CYCLES, LANES), 0) == label, sent, 0.0), axis=0, keepdims=True
            )
        own_sums = jnp.sum(own_rows.astype(jnp.float32), axis=1, keepdims=True)
        earlier[cycle] = jnp.broadcast_to(total / own_sums, (chip_block, LANES))
        for target, position in ((mine_ref, core), (theirs_ref, 1 - core)):
            base = pl.multiple_of(position * block, block)
            scales = [
                later[cycle, :, pl.ds(pl.multiple_of(base + tile * LANES, LANES), LANES)]
                for tile in range(tiles + 1)
            ]
            for batch in range(0, block, BATCH):
                results = []
                for first in range(batch, batch + BATCH, SUBLANES):
                    factor = earlier[cycle, pl.ds(base + first, SUBLANES), :]
                    kept = lane + sublane < LANES - first
                    turned = lax.rem(lane + sublane + first, LANES)
                    rolled = []
                    for tile in range(tiles + 1):
                        column = pl.multiple_of(base + tile * LANES, LANES)
                        value = gram[cycle, pl.ds(base + first, SUBLANES), pl.ds(column, LANES)]
                        value = value * factor * scales[tile]
                        rolled.append(
                            jnp.take_along_axis(value, turned, axis=1, mode="promise_in_bounds")
                        )
                    for tile in range(tiles):
                        results.append(jnp.where(kept, rolled[tile], rolled[tile + 1]))
                at = 0
                for first in range(batch, batch + BATCH, SUBLANES):
                    for tile in range(tiles):
                        target[
                            cycle, first : first + SUBLANES, tile * LANES : (tile + 1) * LANES
                        ] = results[at]
                        at += 1
            if target is theirs_ref:
                continue
            store = pltpu.make_async_copy(
                mine_ref.at[cycle],
                out_ref.at[core * group + offset + cycle, :, pl.ds(phase * lags, lags)],
                sems.at[cycle],
            )
            store.start()
            stores.append(store)
    for copy in stores + fills:
        copy.wait()


def grams(place, counts, sent, whole, windows, choice, sizes, phase, frame_count, ready):
    group_cycles, cycle_dev, offset, count = sizes
    flat = [piece for pieces in windows for piece, _ in pieces]
    chip_block = flat[0].shape[-1]
    block = chip_block // 2
    depth = sum(piece.shape[0] for piece, _ in windows[0]) * CHUNK
    lags = LAG // 2
    width = lags + chip_block
    kernel = functools.partial(
        gram_kernel,
        layout=[[first for _, first in pieces] for pieces in windows],
        choice=choice,
        frame_count=frame_count,
        group=group_cycles,
        offset=offset,
        count=count,
        phase=phase,
        spots=[spot for _, spot in ready],
        chained=whole is not None,
    )
    operands = [place, counts, sent] + flat + [part for part, _ in ready]
    in_specs = [SMEM_SPEC] + [VMEM_SPEC] * (2 + len(flat)) + [ANY_SPEC] * len(ready)
    aliases = {}
    if whole is not None:
        aliases = {len(operands): 0}
        operands.append(whole)
        in_specs.append(ANY_SPEC)
    return pl.pallas_call(
        kernel,
        out_shape=[
            jax.ShapeDtypeStruct((cycle_dev, block, LAG), jnp.float32),
            jax.ShapeDtypeStruct((count, block, lags), jnp.float32),
        ],
        in_specs=in_specs,
        out_specs=[ANY_SPEC, VMEM_SPEC],
        scratch_shapes=[
            pltpu.VMEM((count, block, lags), jnp.float32),
            pltpu.VMEM((count, chip_block + PACKED, width), jnp.float32),
            pltpu.VMEM((count, SUBLANES, width), jnp.float32),
            pltpu.VMEM((count, chip_block, LANES), jnp.float32),
            pltpu.SemaphoreType.DMA((count,)),
            pltpu.SemaphoreType.DMA((max(1, len(ready)),)),
        ],
        input_output_aliases=aliases,
        compiler_params=params(),
        cost_estimate=estimate(
            2 * count * depth * width * chip_block, 4 * count * chip_block * lags
        ),
    )(*operands)


def fill_copies(core, part_refs, spots, out_ref, sems):
    copies = []
    for number, (part_ref, (group, offset, lag)) in enumerate(zip(part_refs, spots)):
        cycles, _, lags = part_ref.shape
        first = (1 - core) * group + offset
        copies.append(
            pltpu.make_async_copy(
                part_ref,
                out_ref.at[pl.ds(first, cycles), :, pl.ds(lag, lags)],
                sems.at[number],
            )
        )
    return copies


def fill_kernel(place_ref, *rest, spots):
    part_refs, out_ref, sems = rest[: len(spots)], rest[-2], rest[-1]
    copies = fill_copies(place_ref[0], part_refs, spots, out_ref, sems)
    for copy in copies:
        copy.start()
    for copy in copies:
        copy.wait()


def fill(place, token, whole, ready):
    parts, spots = zip(*ready)
    return pl.pallas_call(
        functools.partial(fill_kernel, spots=spots),
        out_shape=jax.ShapeDtypeStruct(whole.shape, whole.dtype),
        in_specs=[SMEM_SPEC] + [ANY_SPEC] * (len(parts) + 2),
        out_specs=ANY_SPEC,
        scratch_shapes=[pltpu.SemaphoreType.DMA((len(parts),))],
        input_output_aliases={2 + len(parts): 0},
        compiler_params=params(),
        cost_estimate=estimate(0, 8 * sum(part.size for part in parts)),
    )(place, *parts, token, whole)


def pause_kernel(value_ref, out_ref):
    out_ref[...] = value_ref[...]


def pause(value, weight):
    return pl.pallas_call(
        pause_kernel,
        out_shape=jax.ShapeDtypeStruct(value.shape, value.dtype),
        in_specs=[VMEM_SPEC],
        out_specs=VMEM_SPEC,
        compiler_params=pltpu.CompilerParams(vmem_limit_bytes=1024 * 1024),
        cost_estimate=estimate(weight, 0),
    )(value)


def shifted(value, pairs_down):
    step = 2 * pairs_down
    count = lax.axis_size("frame")
    return lax.ppermute(value, "frame", [(source, source - step) for source in range(step, count)])


def other_pair(value, parity=None):
    count = lax.axis_size("frame")
    sources = [at for at in range(count) if parity is None or at // 2 % 2 == parity]
    return lax.ppermute(value, "frame", [(source, source ^ 2) for source in sources])


def other_core(value):
    count = lax.axis_size("frame")
    return lax.ppermute(value, "frame", [(source, source ^ 1) for source in range(count)])


def along_mod(value, step, odd_pairs=False):
    frames, mods = lax.axis_size("frame"), lax.axis_size("mod")
    pairs = [
        (frame * mods + mod, (frame - 2 * odd_pairs) * mods + (mod + step) % mods)
        for frame in range(frames)
        for mod in range(mods)
        if not odd_pairs or frame // 2 % 2
    ]
    return lax.ppermute(value, ("frame", "mod"), pairs)


def shards(frames, cycle_label, good_pixel):
    mods = lax.axis_size("mod")
    cycle_dev = CYCLES // mods
    group_cycles = cycle_dev // 2
    mod, frame = lax.axis_index("mod"), lax.axis_index("frame")
    core, chip = frame % 2, frame // 2
    block, pix_count = frames.shape
    frame_count = block * lax.axis_size("frame")
    assert LAG == 8 * block and block == LANES and pix_count == CYCLES * CHUNK
    place = jnp.stack([core, chip, mod]).astype(jnp.int32)
    half = group_cycles // 2
    parts = [half, group_cycles - half] if half else [group_cycles]
    offsets = [sum(parts[:number]) for number in range(len(parts))]

    halves = len(parts)
    own_units = halves if OWN_SPLIT else 1
    other = other_core(frames)
    used = jnp.where(good_pixel > 0, cycle_label, CYCLES)
    key, counts, own_frames = rank_pixels(used, frames)
    done = {}

    token = counts

    def tied(value, name):
        nonlocal token
        value, token = lax.optimization_barrier((value, token))
        return value

    def known(name):
        limits = dict(g=halves, s=halves, y=halves, k=mods, o=2)
        return all(int(at) < limits.get(name[0], own_units + halves) for at in name[-1])

    def get(name):
        if name not in done:
            done[name] = make(name[0], name, *(int(at) for at in name[1:]))
        return done[name]

    def make(kind, name, first, second=0):
        if kind == "k":
            joined = [own_frames, other] if first == 0 else [get("k0")[-1]]
            split = first > 0 or own_units > 1
            return order_pixels(place, tied(key, name), counts, joined, first, mods, parts, split)
        if kind == "y":
            return jnp.stack(
                [along_mod(tied(get(f"k{step}")[1 + first], name), step) for step in range(1, mods)]
            )
        if kind == "u":
            if first >= own_units:
                return get(f"y{first - own_units}")
            return get("k0")[1 + first if own_units > 1 else 0][None]
        if kind == "z":
            return shifted(tied(get(f"u{first}"), name), 2)
        if kind == "w":
            return shifted(tied(get(f"z{first}"), name), 2)
        if kind == "x":
            return other_pair(tied(get(f"z{first}"), name))
        if kind == "v":
            return other_pair(tied(get(f"w{first}"), name), 0)
        if kind == "o":
            if first == 0:
                return other_pair(tied(get("k0")[0], name), 1)[None]
            return jnp.stack(
                [along_mod(tied(get(f"k{step}")[0], name), step, True) for step in range(1, mods)]
            )
        if kind == "s":
            return other_core(get(f"g{first}{second}")[1])
        assert kind == "g"
        phase, part = first, second

        def both(letter):
            early = (get(f"{letter}{part}"), 0) if own_units > 1 else (get(f"{letter}0"), offsets[part])
            return [early, (get(f"{letter}{own_units + part}"), 0)]

        if phase == 0:
            neighbour = [(get(f"o{at}"), offsets[part]) for at in range(2)]
            windows, choice = [both("u"), both("z"), neighbour, both("x")], (1, 2, 3)
        else:
            windows = [both(letter) for letter in "uzwxv"]
            choice = (1, 3, 4)
        before = phase * halves + part - 1
        whole = get(f"g{before // halves}{before % halves}")[0] if before >= 0 else None
        filled = [spot(0, at) for at in range(halves)] if phase and not part else []
        sizes = (group_cycles, cycle_dev, offsets[part], parts[part])
        return grams(
            place, tied(counts, name), get(f"u{own_units}"), whole, windows, choice, sizes, phase, frame_count, filled
        )

    def spot(phase, part):
        return get(f"s{phase}{part}"), (group_cycles, offsets[part], phase * (LAG // 2))

    for step, *names in ORDER:
        if step == "pause":
            token = pause(token, *names)
            continue
        for name in filter(known, names):
            value = get(name)
            if step == "wait":
                if isinstance(value, (list, tuple)):
                    head, token = lax.optimization_barrier((value[0], token))
                    done[name] = [head, *value[1:]]
                else:
                    done[name], token = lax.optimization_barrier((value, token))
    whole = get(f"g1{halves - 1}")[0]
    return fill(place, token, whole, [spot(1, part) for part in range(halves)])


def solution(mesh):
    placed = (P("frame", "mod"), P("mod"), P("mod"))
    return jax.shard_map(
        shards, mesh=mesh, in_specs=placed, out_specs=P("mod", "frame", None), check_vma=False
    )
```

```python
import functools

import jax
import jax.numpy as jnp
from jax import lax
from jax.experimental import pallas as pl
from jax.experimental.pallas import tpu as pltpu
from jax.sharding import PartitionSpec as P

CYCLES = 16
LAG = 1024
LANES = 128
SUBLANES = 8
PACKED = 16
BATCH = 64
CHUNK = 256
VMEM_LIMIT = 24 * 1024 * 1024

ORDER = (
    ("start", "o0", "z0", "y0"),
    ("wait", "k1"),
    ("start", "z1"),
    ("wait", "z0"),
    ("pause", 1000000000),
    ("start", "w0", "x0"),
    ("wait", "y0"),
    ("start", "z2"),
    ("wait", "o0"),
    ("start", "x1", "w1"),
    ("wait", "w0"),
    ("start", "v0"),
    ("wait", "z1", "x0"),
    ("start", "y1", "x2", "w2"),
    ("wait", "x1"),
    ("start", "v1", "o1"),
    ("wait", "z2", "y1", "v0", "w1"),
    ("start", "z3"),
    ("pause", 100000000),
    ("pause", 300000000),
    ("pause", 0),
    ("wait", "w0", "x2"),
    ("pause", 100000000),
    ("start", "v2"),
    ("wait", "w2", "v1"),
    ("start", "w3", "x3"),
    ("pause", 300000000),
    ("wait", "o1", "v2", "g00", "w3"),
    ("start", "v3"),
    ("pause", 0),
    ("wait", "x3", "g01"),
    ("pause", 0),
    ("wait", "g10", "v3", "g11"),
)
OWN_SPLIT = True

SMEM_SPEC = pl.BlockSpec(memory_space=pltpu.SMEM)
VMEM_SPEC = pl.BlockSpec(memory_space=pltpu.VMEM)
HBM_SPEC = pl.BlockSpec(memory_space=pltpu.HBM)
ANY_SPEC = pl.BlockSpec(memory_space=pl.ANY)

dot = functools.partial(jnp.dot, preferred_element_type=jnp.float32)


def params():
    return pltpu.CompilerParams(vmem_limit_bytes=VMEM_LIMIT)


def estimate(flops, moved):
    return pl.CostEstimate(flops=flops, bytes_accessed=moved, transcendentals=0)


def ones_where(condition):
    return jnp.where(condition, 1.0, 0.0).astype(jnp.bfloat16)


def iota(shape, dimension):
    return lax.broadcasted_iota(jnp.int32, shape, dimension)


def rank_kernel(label_ref, frames_hbm, key_ref, counts_ref, frames_ref, sem):
    copy = pltpu.make_async_copy(frames_hbm, frames_ref, sem)
    copy.start()
    chunks = label_ref.shape[0] // CHUNK
    rows = chunks * CYCLES
    up, across = iota((rows, rows), 0), iota((rows, rows), 1)
    same = lax.rem(up, CYCLES) == lax.rem(across, CYCLES)
    chunk_before = ones_where(same & (across < up))
    before = ones_where(iota((CHUNK, CHUNK), 0) < iota((CHUNK, CHUNK), 1))
    of_cycle = ones_where(iota((CYCLES, rows), 0) == lax.rem(iota((CYCLES, rows), 1), CYCLES))
    cycle_at = iota((CYCLES, CHUNK), 0)
    labels = [label_ref[pl.ds(at * CHUNK, CHUNK)].reshape(1, CHUNK) for at in range(chunks)]
    used = jnp.concatenate([jnp.where(one == cycle_at, 1.0, 0.0) for one in labels], axis=0)
    member = used.astype(jnp.bfloat16)
    earlier = dot(chunk_before, member).astype(jnp.bfloat16)
    rank = dot(member, before) + dot(earlier, jnp.ones((CHUNK, CHUNK), jnp.bfloat16))
    key_ref[...] = jnp.where(used > 0.0, rank, -1.0)
    per_lane = dot(of_cycle, member).astype(jnp.bfloat16)
    counts_ref[...] = dot(per_lane, jnp.ones((CHUNK, LANES), jnp.bfloat16))
    copy.wait()


def rank_pixels(label, frames):
    rows = label.shape[0] // CHUNK * CYCLES
    return pl.pallas_call(
        rank_kernel,
        out_shape=[
            jax.ShapeDtypeStruct((rows, CHUNK), jnp.float32),
            jax.ShapeDtypeStruct((CYCLES, LANES), jnp.float32),
            jax.ShapeDtypeStruct(frames.shape, frames.dtype),
        ],
        in_specs=[VMEM_SPEC, HBM_SPEC],
        out_specs=[VMEM_SPEC] * 3,
        scratch_shapes=[pltpu.SemaphoreType.DMA],
        compiler_params=params(),
        cost_estimate=estimate(6 * rows * CHUNK * CHUNK, 8 * label.shape[0]),
    )(label, pltpu.with_memory_space_constraint(frames, pltpu.HBM))


def order_kernel(place_ref, key_ref, counts_ref, *rest, step, mods, parts, joined):
    rest = list(rest)
    core, mod = place_ref[0], place_ref[2]
    if joined:
        frames_ref = rest.pop(0)
    else:
        own_ref, other_ref, frames_ref = rest.pop(0), rest.pop(0), rest.pop()
        block = own_ref.shape[0]
        frames_ref[pl.ds(pl.multiple_of(core * block, block), block), :] = own_ref[...]
        frames_ref[pl.ds(pl.multiple_of((1 - core) * block, block), block), :] = other_ref[...]
    frames = frames_ref[...]
    all_ref, part_refs = rest[0], rest[1:]
    chunks = key_ref.shape[0] // CYCLES
    per_cycle = frames.shape[1] // CYCLES
    first_cycle = (lax.rem(mod + step, mods) * 2 + core) * sum(parts)
    if step:
        row = parts[0] * per_cycle
        sent = jnp.concatenate([counts_ref[...]] * (frames.shape[0] // LANES), axis=1)
        part_refs[0][row : row + CYCLES, :] = sent.astype(jnp.bfloat16)
    slots = [
        (iota((PACKED, CHUNK), 0) + first).astype(jnp.float32).astype(jnp.bfloat16)
        for first in range(0, per_cycle, PACKED)
    ]
    one = jnp.ones((PACKED, CHUNK), jnp.bfloat16)
    zero = jnp.zeros((PACKED, CHUNK), jnp.bfloat16)
    spots = [(number, at) for number, part in enumerate(parts) for at in range(part)]
    for cycle, (number, at) in enumerate(spots):
        tiles = []
        for chunk in range(chunks):
            key = key_ref[pl.ds(chunk * CYCLES + first_cycle + cycle, 1), :]
            key = jnp.broadcast_to(key, (PACKED, CHUNK)).astype(jnp.bfloat16)
            tiles.append(
                jnp.concatenate([jnp.where(key == slot, one, zero) for slot in slots], axis=0)
            )
        picked = lax.dot_general(
            jnp.concatenate(tiles, axis=1),
            frames,
            (((1,), (1,)), ((), ())),
            preferred_element_type=jnp.float32,
        ).astype(jnp.bfloat16)
        all_ref[cycle * per_cycle : (cycle + 1) * per_cycle, :] = picked
        if part_refs:
            part_refs[number][at * per_cycle : (at + 1) * per_cycle, :] = picked


def order_pixels(place, key, counts, frames, step, mods, parts, split):
    joined = len(frames) == 1
    chip_block = frames[0].shape[0] * (1 if joined else 2)
    pix_count = frames[0].shape[1]
    per_cycle = pix_count // CYCLES
    heights = [part * per_cycle for part in [sum(parts)] + (list(parts) if split else [])]
    if step:
        heights[1] += CYCLES
    out_shape = [jax.ShapeDtypeStruct((height, chip_block), jnp.bfloat16) for height in heights]
    if not joined:
        out_shape.append(jax.ShapeDtypeStruct((chip_block, pix_count), jnp.bfloat16))
    return pl.pallas_call(
        functools.partial(order_kernel, step=step, mods=mods, parts=parts, joined=joined),
        out_shape=out_shape,
        in_specs=[SMEM_SPEC] + [VMEM_SPEC] * (2 + len(frames)),
        out_specs=[VMEM_SPEC] * len(out_shape),
        compiler_params=params(),
        cost_estimate=estimate(
            2 * sum(parts) * per_cycle * pix_count * chip_block, 2 * pix_count * chip_block
        ),
    )(place, key, counts, *frames)


def gram_kernel(place_ref, counts_ref, sent_ref, *rest, layout, choice, frame_count, group, offset, count, phase, spots, chained):
    rest = list(rest)
    windows = [[(rest.pop(0), first) for first in pieces] for pieces in layout]
    ready_refs = [rest.pop(0) for _ in spots]
    if chained:
        rest.pop(0)
    out_ref, theirs_ref, mine_ref, gram, later, earlier, sems, fill_sems = rest
    core, chip, mod = place_ref[0], place_ref[1], place_ref[2]
    fills = fill_copies(core, ready_refs, spots, out_ref, fill_sems)
    for copy in fills:
        copy.start()
    _, block, lags = theirs_ref.shape
    chip_block = 2 * block
    per_cycle = CHUNK
    lane, sublane = iota((SUBLANES, LANES), 1), iota((SUBLANES, LANES), 0)
    tiles = lags // LANES
    stores = []
    for cycle in range(count):

        def rows_of(number):
            return jnp.concatenate(
                [
                    ref[source, (first + cycle) * per_cycle : (first + cycle + 1) * per_cycle, :]
                    for ref, first in windows[number]
                    for source in range(ref.shape[0])
                ],
                axis=0,
            )

        columns = [rows_of(number) for number in range(len(windows))]
        own = columns[0]
        at, even, odd = choice
        chosen = jnp.where(lax.rem(chip, 2) == 0, columns[even], columns[odd])
        columns = [
            value
            for number, value in enumerate(columns)
            if number not in (even, odd) and (number or phase == 0)
        ]
        columns.insert(at, chosen)
        whole = jnp.concatenate(columns, axis=1)
        depth, width = whole.shape
        own_rows = own.T
        ones = jnp.ones((PACKED, depth), jnp.bfloat16)
        gram[cycle] = dot(jnp.concatenate([own_rows, ones], axis=0), whole)
        sums = gram[cycle, chip_block : chip_block + SUBLANES, :]
        frame_at = chip * chip_block + phase * lags + iota((SUBLANES, width), 1)
        later[cycle] = jnp.where(frame_at < frame_count, 1.0 / sums, 0.0)
        label = (mod * 2 + core) * group + offset + cycle
        total = counts_ref[pl.ds(label, 1), :]
        for source in range(sent_ref.shape[0]):
            sent = sent_ref[source, sent_ref.shape[1] - CYCLES :, :LANES].astype(jnp.float32)
            total += jnp.sum(
                jnp.where(iota((CYCLES, LANES), 0) == label, sent, 0.0), axis=0, keepdims=True
            )
        own_sums = jnp.sum(own_rows.astype(jnp.float32), axis=1, keepdims=True)
        earlier[cycle] = jnp.broadcast_to(total / own_sums, (chip_block, LANES))
        for target, position in ((mine_ref, core), (theirs_ref, 1 - core)):
            base = pl.multiple_of(position * block, block)
            scales = [
                later[cycle, :, pl.ds(pl.multiple_of(base + tile * LANES, LANES), LANES)]
                for tile in range(tiles + 1)
            ]
            for batch in range(0, block, BATCH):
                results = []
                for first in range(batch, batch + BATCH, SUBLANES):
                    factor = earlier[cycle, pl.ds(base + first, SUBLANES), :]
                    kept = lane + sublane < LANES - first
                    turned = lax.rem(lane + sublane + first, LANES)
                    rolled = []
                    for tile in range(tiles + 1):
                        column = pl.multiple_of(base + tile * LANES, LANES)
                        value = gram[cycle, pl.ds(base + first, SUBLANES), pl.ds(column, LANES)]
                        value = value * factor * scales[tile]
                        rolled.append(
                            jnp.take_along_axis(value, turned, axis=1, mode="promise_in_bounds")
                        )
                    for tile in range(tiles):
                        results.append(jnp.where(kept, rolled[tile], rolled[tile + 1]))
                at = 0
                for first in range(batch, batch + BATCH, SUBLANES):
                    for tile in range(tiles):
                        target[
                            cycle, first : first + SUBLANES, tile * LANES : (tile + 1) * LANES
                        ] = results[at]
                        at += 1
            if target is theirs_ref:
                continue
            store = pltpu.make_async_copy(
                mine_ref.at[cycle],
                out_ref.at[core * group + offset + cycle, :, pl.ds(phase * lags, lags)],
                sems.at[cycle],
            )
            store.start()
            stores.append(store)
    for copy in stores + fills:
        copy.wait()


def grams(place, counts, sent, whole, windows, choice, sizes, phase, frame_count, ready):
    group_cycles, cycle_dev, offset, count = sizes
    flat = [piece for pieces in windows for piece, _ in pieces]
    chip_block = flat[0].shape[-1]
    block = chip_block // 2
    depth = sum(piece.shape[0] for piece, _ in windows[0]) * CHUNK
    lags = LAG // 2
    width = lags + chip_block
    kernel = functools.partial(
        gram_kernel,
        layout=[[first for _, first in pieces] for pieces in windows],
        choice=choice,
        frame_count=frame_count,
        group=group_cycles,
        offset=offset,
        count=count,
        phase=phase,
        spots=[spot for _, spot in ready],
        chained=whole is not None,
    )
    operands = [place, counts, sent] + flat + [part for part, _ in ready]
    in_specs = [SMEM_SPEC] + [VMEM_SPEC] * (2 + len(flat)) + [ANY_SPEC] * len(ready)
    aliases = {}
    if whole is not None:
        aliases = {len(operands): 0}
        operands.append(whole)
        in_specs.append(ANY_SPEC)
    return pl.pallas_call(
        kernel,
        out_shape=[
            jax.ShapeDtypeStruct((cycle_dev, block, LAG), jnp.float32),
            jax.ShapeDtypeStruct((count, block, lags), jnp.float32),
        ],
        in_specs=in_specs,
        out_specs=[ANY_SPEC, VMEM_SPEC],
        scratch_shapes=[
            pltpu.VMEM((count, block, lags), jnp.float32),
            pltpu.VMEM((count, chip_block + PACKED, width), jnp.float32),
            pltpu.VMEM((count, SUBLANES, width), jnp.float32),
            pltpu.VMEM((count, chip_block, LANES), jnp.float32),
            pltpu.SemaphoreType.DMA((count,)),
            pltpu.SemaphoreType.DMA((max(1, len(ready)),)),
        ],
        input_output_aliases=aliases,
        compiler_params=params(),
        cost_estimate=estimate(0, 0),
    )(*operands)


def fill_copies(core, part_refs, spots, out_ref, sems):
    copies = []
    for number, (part_ref, (group, offset, lag)) in enumerate(zip(part_refs, spots)):
        cycles, _, lags = part_ref.shape
        first = (1 - core) * group + offset
        copies.append(
            pltpu.make_async_copy(
                part_ref,
                out_ref.at[pl.ds(first, cycles), :, pl.ds(lag, lags)],
                sems.at[number],
            )
        )
    return copies


def fill_kernel(place_ref, *rest, spots):
    part_refs, out_ref, sems = rest[: len(spots)], rest[-2], rest[-1]
    copies = fill_copies(place_ref[0], part_refs, spots, out_ref, sems)
    for copy in copies:
        copy.start()
    for copy in copies:
        copy.wait()


def fill(place, token, whole, ready):
    parts, spots = zip(*ready)
    return pl.pallas_call(
        functools.partial(fill_kernel, spots=spots),
        out_shape=jax.ShapeDtypeStruct(whole.shape, whole.dtype),
        in_specs=[SMEM_SPEC] + [ANY_SPEC] * (len(parts) + 2),
        out_specs=ANY_SPEC,
        scratch_shapes=[pltpu.SemaphoreType.DMA((len(parts),))],
        input_output_aliases={2 + len(parts): 0},
        compiler_params=params(),
        cost_estimate=estimate(0, 8 * sum(part.size for part in parts)),
    )(place, *parts, token, whole)


def pause_kernel(value_ref, out_ref):
    out_ref[...] = value_ref[...]


def pause(value, weight):
    return pl.pallas_call(
        pause_kernel,
        out_shape=jax.ShapeDtypeStruct(value.shape, value.dtype),
        in_specs=[VMEM_SPEC],
        out_specs=VMEM_SPEC,
        compiler_params=pltpu.CompilerParams(vmem_limit_bytes=1024 * 1024),
        cost_estimate=estimate(weight, 0),
    )(value)


def shifted(value, pairs_down):
    step = 2 * pairs_down
    count = lax.axis_size("frame")
    return lax.ppermute(value, "frame", [(source, source - step) for source in range(step, count)])


def other_pair(value, parity=None):
    count = lax.axis_size("frame")
    sources = [at for at in range(count) if parity is None or at // 2 % 2 == parity]
    return lax.ppermute(value, "frame", [(source, source ^ 2) for source in sources])


def other_core(value):
    count = lax.axis_size("frame")
    return lax.ppermute(value, "frame", [(source, source ^ 1) for source in range(count)])


def along_mod(value, step, odd_pairs=False):
    frames, mods = lax.axis_size("frame"), lax.axis_size("mod")
    pairs = [
        (frame * mods + mod, (frame - 2 * odd_pairs) * mods + (mod + step) % mods)
        for frame in range(frames)
        for mod in range(mods)
        if not odd_pairs or frame // 2 % 2
    ]
    return lax.ppermute(value, ("frame", "mod"), pairs)


def shards(frames, cycle_label, good_pixel):
    mods = lax.axis_size("mod")
    cycle_dev = CYCLES // mods
    group_cycles = cycle_dev // 2
    mod, frame = lax.axis_index("mod"), lax.axis_index("frame")
    core, chip = frame % 2, frame // 2
    block, pix_count = frames.shape
    frame_count = block * lax.axis_size("frame")
    assert LAG == 8 * block and block == LANES and pix_count == CYCLES * CHUNK
    place = jnp.stack([core, chip, mod]).astype(jnp.int32)
    half = group_cycles // 2
    parts = [half, group_cycles - half] if half else [group_cycles]
    offsets = [sum(parts[:number]) for number in range(len(parts))]

    halves = len(parts)
    own_units = halves if OWN_SPLIT else 1
    other = other_core(frames)
    used = jnp.where(good_pixel > 0, cycle_label, CYCLES)
    key, counts, own_frames = rank_pixels(used, frames)
    done = {}

    token = counts

    def tied(value, name):
        nonlocal token
        value, token = lax.optimization_barrier((value, token))
        return value

    def known(name):
        limits = dict(g=halves, s=halves, y=halves, k=mods, o=2)
        return all(int(at) < limits.get(name[0], own_units + halves) for at in name[-1])

    def get(name):
        if name not in done:
            done[name] = make(name[0], name, *(int(at) for at in name[1:]))
        return done[name]

    def make(kind, name, first, second=0):
        if kind == "k":
            joined = [own_frames, other] if first == 0 else [get("k0")[-1]]
            split = first > 0 or own_units > 1
            return order_pixels(place, tied(key, name), counts, joined, first, mods, parts, split)
        if kind == "y":
            return jnp.stack(
                [along_mod(tied(get(f"k{step}")[1 + first], name), step) for step in range(1, mods)]
            )
        if kind == "u":
            if first >= own_units:
                return get(f"y{first - own_units}")
            return get("k0")[1 + first if own_units > 1 else 0][None]
        if kind == "z":
            return shifted(tied(get(f"u{first}"), name), 2)
        if kind == "w":
            return shifted(tied(get(f"z{first}"), name), 2)
        if kind == "x":
            return other_pair(tied(get(f"z{first}"), name))
        if kind == "v":
            return other_pair(tied(get(f"w{first}"), name), 0)
        if kind == "o":
            if first == 0:
                return other_pair(tied(get("k0")[0], name), 1)[None]
            return jnp.stack(
                [along_mod(tied(get(f"k{step}")[0], name), step, True) for step in range(1, mods)]
            )
        if kind == "s":
            return other_core(get(f"g{first}{second}")[1])
        assert kind == "g"
        phase, part = first, second

        def both(letter):
            early = (get(f"{letter}{part}"), 0) if own_units > 1 else (get(f"{letter}0"), offsets[part])
            return [early, (get(f"{letter}{own_units + part}"), 0)]

        if phase == 0:
            neighbour = [(get(f"o{at}"), offsets[part]) for at in range(2)]
            windows, choice = [both("u"), both("z"), neighbour, both("x")], (1, 2, 3)
        else:
            windows = [both(letter) for letter in "uzwxv"]
            choice = (1, 3, 4)
        before = phase * halves + part - 1
        whole = get(f"g{before // halves}{before % halves}")[0] if before >= 0 else None
        filled = []
        sizes = (group_cycles, cycle_dev, offsets[part], parts[part])
        return grams(
            place, tied(counts, name), get(f"u{own_units}"), whole, windows, choice, sizes, phase, frame_count, filled
        )

    def spot(phase, part):
        return get(f"s{phase}{part}"), (group_cycles, offsets[part], phase * (LAG // 2))

    for step, *names in ORDER:
        if step == "pause":
            token = pause(token, *names)
            continue
        for name in filter(known, names):
            value = get(name)
            if step == "wait":
                if name[0] == "g":
                    theirs, token = lax.optimization_barrier((value[1], token))
                    done[name] = [value[0], theirs]
                elif isinstance(value, (list, tuple)):
                    head, token = lax.optimization_barrier((value[0], token))
                    done[name] = [head, *value[1:]]
                else:
                    done[name], token = lax.optimization_barrier((value, token))
    whole = get(f"g1{halves - 1}")[0]
    spots = [spot(phase, part) for phase in range(2) for part in range(halves)]
    return fill(place, token, whole, spots)


def solution(mesh):
    placed = (P("frame", "mod"), P("mod"), P("mod"))
    return jax.shard_map(
        shards, mesh=mesh, in_specs=placed, out_specs=P("mod", "frame", None), check_vma=False
    )
```

```python
import functools

import jax
import jax.numpy as jnp
from jax import lax
from jax.experimental import pallas as pl
from jax.experimental.pallas import tpu as pltpu
from jax.sharding import PartitionSpec as P

CYCLES = 16
LAG = 1024
LANES = 128
SUBLANES = 8
PACKED = 16
BATCH = 64
CHUNK = 256
VMEM_LIMIT = 24 * 1024 * 1024

ORDER = (
    ("start", "o0", "z0", "y0"),
    ("wait", "k1"),
    ("start", "z1"),
    ("wait", "z0"),
    ("pause", 1000000000),
    ("start", "w0", "x0"),
    ("wait", "y0"),
    ("start", "z2"),
    ("wait", "o0"),
    ("start", "x1", "w1"),
    ("wait", "w0"),
    ("start", "v0"),
    ("wait", "z1", "x0"),
    ("start", "y1", "x2", "w2"),
    ("wait", "x1"),
    ("start", "v1", "o1"),
    ("wait", "z2", "y1", "v0", "w1"),
    ("start", "z3"),
    ("pause", 100000000),
    ("pause", 300000000),
    ("pause", 0),
    ("wait", "w0", "x2"),
    ("pause", 100000000),
    ("start", "v2"),
    ("wait", "w2", "v1"),
    ("start", "w3", "x3"),
    ("pause", 300000000),
    ("wait", "o1", "v2", "g00", "w3"),
    ("start", "v3"),
    ("pause", 0),
    ("wait", "x3", "g01"),
    ("pause", 0),
    ("wait", "g10", "v3", "g11"),
)
OWN_SPLIT = True

SMEM_SPEC = pl.BlockSpec(memory_space=pltpu.SMEM)
VMEM_SPEC = pl.BlockSpec(memory_space=pltpu.VMEM)
HBM_SPEC = pl.BlockSpec(memory_space=pltpu.HBM)
ANY_SPEC = pl.BlockSpec(memory_space=pl.ANY)

dot = functools.partial(jnp.dot, preferred_element_type=jnp.float32)


def params():
    return pltpu.CompilerParams(vmem_limit_bytes=VMEM_LIMIT)


def estimate(flops, moved):
    return pl.CostEstimate(flops=flops, bytes_accessed=moved, transcendentals=0)


def ones_where(condition):
    return jnp.where(condition, 1.0, 0.0).astype(jnp.bfloat16)


def iota(shape, dimension):
    return lax.broadcasted_iota(jnp.int32, shape, dimension)


def rank_kernel(label_ref, frames_hbm, key_ref, counts_ref, frames_ref, sem):
    copy = pltpu.make_async_copy(frames_hbm, frames_ref, sem)
    copy.start()
    chunks = label_ref.shape[0] // CHUNK
    rows = chunks * CYCLES
    up, across = iota((rows, rows), 0), iota((rows, rows), 1)
    same = lax.rem(up, CYCLES) == lax.rem(across, CYCLES)
    chunk_before = ones_where(same & (across < up))
    before = ones_where(iota((CHUNK, CHUNK), 0) < iota((CHUNK, CHUNK), 1))
    of_cycle = ones_where(iota((CYCLES, rows), 0) == lax.rem(iota((CYCLES, rows), 1), CYCLES))
    cycle_at = iota((CYCLES, CHUNK), 0)
    labels = [label_ref[pl.ds(at * CHUNK, CHUNK)].reshape(1, CHUNK) for at in range(chunks)]
    used = jnp.concatenate([jnp.where(one == cycle_at, 1.0, 0.0) for one in labels], axis=0)
    member = used.astype(jnp.bfloat16)
    earlier = dot(chunk_before, member).astype(jnp.bfloat16)
    rank = dot(member, before) + dot(earlier, jnp.ones((CHUNK, CHUNK), jnp.bfloat16))
    key_ref[...] = jnp.where(used > 0.0, rank, -1.0)
    per_lane = dot(of_cycle, member).astype(jnp.bfloat16)
    counts_ref[...] = dot(per_lane, jnp.ones((CHUNK, LANES), jnp.bfloat16))
    copy.wait()


def rank_pixels(label, frames):
    rows = label.shape[0] // CHUNK * CYCLES
    return pl.pallas_call(
        rank_kernel,
        out_shape=[
            jax.ShapeDtypeStruct((rows, CHUNK), jnp.float32),
            jax.ShapeDtypeStruct((CYCLES, LANES), jnp.float32),
            jax.ShapeDtypeStruct(frames.shape, frames.dtype),
        ],
        in_specs=[VMEM_SPEC, HBM_SPEC],
        out_specs=[VMEM_SPEC] * 3,
        scratch_shapes=[pltpu.SemaphoreType.DMA],
        compiler_params=params(),
        cost_estimate=estimate(6 * rows * CHUNK * CHUNK, 8 * label.shape[0]),
    )(label, pltpu.with_memory_space_constraint(frames, pltpu.HBM))


def order_kernel(place_ref, key_ref, counts_ref, *rest, step, mods, parts, joined):
    rest = list(rest)
    core, mod = place_ref[0], place_ref[2]
    if joined:
        frames_ref = rest.pop(0)
    else:
        own_ref, other_ref, frames_ref = rest.pop(0), rest.pop(0), rest.pop()
        block = own_ref.shape[0]
        frames_ref[pl.ds(pl.multiple_of(core * block, block), block), :] = own_ref[...]
        frames_ref[pl.ds(pl.multiple_of((1 - core) * block, block), block), :] = other_ref[...]
    frames = frames_ref[...]
    all_ref, part_refs = rest[0], rest[1:]
    chunks = key_ref.shape[0] // CYCLES
    per_cycle = frames.shape[1] // CYCLES
    first_cycle = (lax.rem(mod + step, mods) * 2 + core) * sum(parts)
    if step:
        row = parts[0] * per_cycle
        sent = jnp.concatenate([counts_ref[...]] * (frames.shape[0] // LANES), axis=1)
        part_refs[0][row : row + CYCLES, :] = sent.astype(jnp.bfloat16)
    slots = [
        (iota((PACKED, CHUNK), 0) + first).astype(jnp.float32).astype(jnp.bfloat16)
        for first in range(0, per_cycle, PACKED)
    ]
    one = jnp.ones((PACKED, CHUNK), jnp.bfloat16)
    zero = jnp.zeros((PACKED, CHUNK), jnp.bfloat16)
    spots = [(number, at) for number, part in enumerate(parts) for at in range(part)]
    for cycle, (number, at) in enumerate(spots):
        tiles = []
        for chunk in range(chunks):
            key = key_ref[pl.ds(chunk * CYCLES + first_cycle + cycle, 1), :]
            key = jnp.broadcast_to(key, (PACKED, CHUNK)).astype(jnp.bfloat16)
            tiles.append(
                jnp.concatenate([jnp.where(key == slot, one, zero) for slot in slots], axis=0)
            )
        picked = lax.dot_general(
            jnp.concatenate(tiles, axis=1),
            frames,
            (((1,), (1,)), ((), ())),
            preferred_element_type=jnp.float32,
        ).astype(jnp.bfloat16)
        all_ref[cycle * per_cycle : (cycle + 1) * per_cycle, :] = picked
        if part_refs:
            part_refs[number][at * per_cycle : (at + 1) * per_cycle, :] = picked


def order_pixels(place, key, counts, frames, step, mods, parts, split):
    joined = len(frames) == 1
    chip_block = frames[0].shape[0] * (1 if joined else 2)
    pix_count = frames[0].shape[1]
    per_cycle = pix_count // CYCLES
    heights = [part * per_cycle for part in [sum(parts)] + (list(parts) if split else [])]
    if step:
        heights[1] += CYCLES
    out_shape = [jax.ShapeDtypeStruct((height, chip_block), jnp.bfloat16) for height in heights]
    if not joined:
        out_shape.append(jax.ShapeDtypeStruct((chip_block, pix_count), jnp.bfloat16))
    return pl.pallas_call(
        functools.partial(order_kernel, step=step, mods=mods, parts=parts, joined=joined),
        out_shape=out_shape,
        in_specs=[SMEM_SPEC] + [VMEM_SPEC] * (2 + len(frames)),
        out_specs=[VMEM_SPEC] * len(out_shape),
        compiler_params=params(),
        cost_estimate=estimate(
            2 * sum(parts) * per_cycle * pix_count * chip_block, 2 * pix_count * chip_block
        ),
    )(place, key, counts, *frames)


def gram_kernel(place_ref, counts_ref, sent_ref, *rest, layout, choice, frame_count, group, offset, count, phase, spots, chained):
    rest = list(rest)
    windows = [[(rest.pop(0), first) for first in pieces] for pieces in layout]
    ready_refs = [rest.pop(0) for _ in spots]
    if chained:
        rest.pop(0)
    out_ref, theirs_ref, mine_ref, gram, later, earlier, sems, fill_sems = rest
    core, chip, mod = place_ref[0], place_ref[1], place_ref[2]
    fills = fill_copies(core, ready_refs, spots, out_ref, fill_sems)
    for copy in fills:
        copy.start()
    _, block, lags = theirs_ref.shape
    chip_block = 2 * block
    per_cycle = CHUNK
    lane, sublane = iota((SUBLANES, LANES), 1), iota((SUBLANES, LANES), 0)
    tiles = lags // LANES
    skews = [
        (lane + sublane < LANES - first, (lane + sublane + first) & (LANES - 1))
        for first in range(0, block, SUBLANES)
    ]
    stores = []
    for cycle in range(count):

        def rows_of(number):
            return jnp.concatenate(
                [
                    ref[source, (first + cycle) * per_cycle : (first + cycle + 1) * per_cycle, :]
                    for ref, first in windows[number]
                    for source in range(ref.shape[0])
                ],
                axis=0,
            )

        columns = [rows_of(number) for number in range(len(windows))]
        own = columns[0]
        at, even, odd = choice
        chosen = jnp.where(lax.rem(chip, 2) == 0, columns[even], columns[odd])
        columns = [
            value
            for number, value in enumerate(columns)
            if number not in (even, odd) and (number or phase == 0)
        ]
        columns.insert(at, chosen)
        whole = jnp.concatenate(columns, axis=1)
        depth, width = whole.shape
        own_rows = own.T
        ones = jnp.ones((PACKED, depth), jnp.bfloat16)
        gram[cycle] = dot(jnp.concatenate([own_rows, ones], axis=0), whole)
        sums = gram[cycle, chip_block : chip_block + SUBLANES, :]
        frame_at = chip * chip_block + phase * lags + iota((SUBLANES, width), 1)
        later[cycle] = jnp.where(frame_at < frame_count, 1.0 / sums, 0.0)
        label = (mod * 2 + core) * group + offset + cycle
        total = counts_ref[pl.ds(label, 1), :]
        for source in range(sent_ref.shape[0]):
            sent = sent_ref[source, sent_ref.shape[1] - CYCLES :, :LANES].astype(jnp.float32)
            total += jnp.sum(
                jnp.where(iota((CYCLES, LANES), 0) == label, sent, 0.0), axis=0, keepdims=True
            )
        own_sums = jnp.sum(own_rows.astype(jnp.float32), axis=1, keepdims=True)
        earlier[cycle] = jnp.broadcast_to(total / own_sums, (chip_block, LANES))
        for target, position in ((mine_ref, core), (theirs_ref, 1 - core)):
            base = pl.multiple_of(position * block, block)
            scales = [
                later[cycle, :, pl.ds(pl.multiple_of(base + tile * LANES, LANES), LANES)]
                for tile in range(tiles + 1)
            ]
            for batch in range(0, block, BATCH):
                results = []
                for first in range(batch, batch + BATCH, SUBLANES):
                    factor = earlier[cycle, pl.ds(base + first, SUBLANES), :]
                    kept, turned = skews[first // SUBLANES]
                    rolled = []
                    for tile in range(tiles + 1):
                        column = pl.multiple_of(base + tile * LANES, LANES)
                        value = gram[cycle, pl.ds(base + first, SUBLANES), pl.ds(column, LANES)]
                        value = value * factor * scales[tile]
                        rolled.append(
                            jnp.take_along_axis(value, turned, axis=1, mode="promise_in_bounds")
                        )
                    for tile in range(tiles):
                        results.append(jnp.where(kept, rolled[tile], rolled[tile + 1]))
                at = 0
                for first in range(batch, batch + BATCH, SUBLANES):
                    for tile in range(tiles):
                        target[
                            cycle, first : first + SUBLANES, tile * LANES : (tile + 1) * LANES
                        ] = results[at]
                        at += 1
            if target is theirs_ref:
                continue
            store = pltpu.make_async_copy(
                mine_ref.at[cycle],
                out_ref.at[core * group + offset + cycle, :, pl.ds(phase * lags, lags)],
                sems.at[cycle],
            )
            store.start()
            stores.append(store)
    for copy in stores + fills:
        copy.wait()


def grams(place, counts, sent, whole, windows, choice, sizes, phase, frame_count, ready):
    group_cycles, cycle_dev, offset, count = sizes
    flat = [piece for pieces in windows for piece, _ in pieces]
    chip_block = flat[0].shape[-1]
    block = chip_block // 2
    depth = sum(piece.shape[0] for piece, _ in windows[0]) * CHUNK
    lags = LAG // 2
    width = lags + chip_block
    kernel = functools.partial(
        gram_kernel,
        layout=[[first for _, first in pieces] for pieces in windows],
        choice=choice,
        frame_count=frame_count,
        group=group_cycles,
        offset=offset,
        count=count,
        phase=phase,
        spots=[spot for _, spot in ready],
        chained=whole is not None,
    )
    operands = [place, counts, sent] + flat + [part for part, _ in ready]
    in_specs = [SMEM_SPEC] + [VMEM_SPEC] * (2 + len(flat)) + [ANY_SPEC] * len(ready)
    aliases = {}
    if whole is not None:
        aliases = {len(operands): 0}
        operands.append(whole)
        in_specs.append(ANY_SPEC)
    return pl.pallas_call(
        kernel,
        out_shape=[
            jax.ShapeDtypeStruct((cycle_dev, block, LAG), jnp.float32),
            jax.ShapeDtypeStruct((count, block, lags), jnp.float32),
        ],
        in_specs=in_specs,
        out_specs=[ANY_SPEC, VMEM_SPEC],
        scratch_shapes=[
            pltpu.VMEM((count, block, lags), jnp.float32),
            pltpu.VMEM((count, chip_block + PACKED, width), jnp.float32),
            pltpu.VMEM((count, SUBLANES, width), jnp.float32),
            pltpu.VMEM((count, chip_block, LANES), jnp.float32),
            pltpu.SemaphoreType.DMA((count,)),
            pltpu.SemaphoreType.DMA((max(1, len(ready)),)),
        ],
        input_output_aliases=aliases,
        compiler_params=params(),
        cost_estimate=estimate(0, 0),
    )(*operands)


def fill_copies(core, part_refs, spots, out_ref, sems):
    copies = []
    for number, (part_ref, (group, offset, lag)) in enumerate(zip(part_refs, spots)):
        cycles, _, lags = part_ref.shape
        first = (1 - core) * group + offset
        copies.append(
            pltpu.make_async_copy(
                part_ref,
                out_ref.at[pl.ds(first, cycles), :, pl.ds(lag, lags)],
                sems.at[number],
            )
        )
    return copies


def fill_kernel(place_ref, *rest, spots):
    part_refs, out_ref, sems = rest[: len(spots)], rest[-2], rest[-1]
    copies = fill_copies(place_ref[0], part_refs, spots, out_ref, sems)
    for copy in copies:
        copy.start()
    for copy in copies:
        copy.wait()


def fill(place, token, whole, ready):
    parts, spots = zip(*ready)
    return pl.pallas_call(
        functools.partial(fill_kernel, spots=spots),
        out_shape=jax.ShapeDtypeStruct(whole.shape, whole.dtype),
        in_specs=[SMEM_SPEC] + [ANY_SPEC] * (len(parts) + 2),
        out_specs=ANY_SPEC,
        scratch_shapes=[pltpu.SemaphoreType.DMA((len(parts),))],
        input_output_aliases={2 + len(parts): 0},
        compiler_params=params(),
        cost_estimate=estimate(0, 8 * sum(part.size for part in parts)),
    )(place, *parts, token, whole)


def pause_kernel(value_ref, out_ref):
    out_ref[...] = value_ref[...]


def pause(value, weight):
    return pl.pallas_call(
        pause_kernel,
        out_shape=jax.ShapeDtypeStruct(value.shape, value.dtype),
        in_specs=[VMEM_SPEC],
        out_specs=VMEM_SPEC,
        compiler_params=pltpu.CompilerParams(vmem_limit_bytes=1024 * 1024),
        cost_estimate=estimate(weight, 0),
    )(value)


def shifted(value, pairs_down):
    step = 2 * pairs_down
    count = lax.axis_size("frame")
    return lax.ppermute(value, "frame", [(source, source - step) for source in range(step, count)])


def other_pair(value, parity=None):
    count = lax.axis_size("frame")
    sources = [at for at in range(count) if parity is None or at // 2 % 2 == parity]
    return lax.ppermute(value, "frame", [(source, source ^ 2) for source in sources])


def other_core(value):
    count = lax.axis_size("frame")
    return lax.ppermute(value, "frame", [(source, source ^ 1) for source in range(count)])


def along_mod(value, step, odd_pairs=False):
    frames, mods = lax.axis_size("frame"), lax.axis_size("mod")
    pairs = [
        (frame * mods + mod, (frame - 2 * odd_pairs) * mods + (mod + step) % mods)
        for frame in range(frames)
        for mod in range(mods)
        if not odd_pairs or frame // 2 % 2
    ]
    return lax.ppermute(value, ("frame", "mod"), pairs)


def shards(frames, cycle_label, good_pixel):
    mods = lax.axis_size("mod")
    cycle_dev = CYCLES // mods
    group_cycles = cycle_dev // 2
    mod, frame = lax.axis_index("mod"), lax.axis_index("frame")
    core, chip = frame % 2, frame // 2
    block, pix_count = frames.shape
    frame_count = block * lax.axis_size("frame")
    assert LAG == 8 * block and block == LANES and pix_count == CYCLES * CHUNK
    place = jnp.stack([core, chip, mod]).astype(jnp.int32)
    half = group_cycles // 2
    parts = [half, group_cycles - half] if half else [group_cycles]
    offsets = [sum(parts[:number]) for number in range(len(parts))]

    halves = len(parts)
    own_units = halves if OWN_SPLIT else 1
    other = other_core(frames)
    used = jnp.where(good_pixel > 0, cycle_label, CYCLES)
    key, counts, own_frames = rank_pixels(used, frames)
    done = {}

    token = counts

    def tied(value, name):
        nonlocal token
        value, token = lax.optimization_barrier((value, token))
        return value

    def known(name):
        limits = dict(g=halves, s=halves, y=halves, k=mods, o=2)
        return all(int(at) < limits.get(name[0], own_units + halves) for at in name[-1])

    def get(name):
        if name not in done:
            done[name] = make(name[0], name, *(int(at) for at in name[1:]))
        return done[name]

    def make(kind, name, first, second=0):
        if kind == "k":
            joined = [own_frames, other] if first == 0 else [get("k0")[-1]]
            split = first > 0 or own_units > 1
            return order_pixels(place, tied(key, name), counts, joined, first, mods, parts, split)
        if kind == "y":
            return jnp.stack(
                [along_mod(tied(get(f"k{step}")[1 + first], name), step) for step in range(1, mods)]
            )
        if kind == "u":
            if first >= own_units:
                return get(f"y{first - own_units}")
            return get("k0")[1 + first if own_units > 1 else 0][None]
        if kind == "z":
            return shifted(tied(get(f"u{first}"), name), 2)
        if kind == "w":
            return shifted(tied(get(f"z{first}"), name), 2)
        if kind == "x":
            return other_pair(tied(get(f"z{first}"), name))
        if kind == "v":
            return other_pair(tied(get(f"w{first}"), name), 0)
        if kind == "o":
            if first == 0:
                return other_pair(tied(get("k0")[0], name), 1)[None]
            return jnp.stack(
                [along_mod(tied(get(f"k{step}")[0], name), step, True) for step in range(1, mods)]
            )
        if kind == "s":
            return other_core(get(f"g{first}{second}")[1])
        assert kind == "g"
        phase, part = first, second

        def both(letter):
            early = (get(f"{letter}{part}"), 0) if own_units > 1 else (get(f"{letter}0"), offsets[part])
            return [early, (get(f"{letter}{own_units + part}"), 0)]

        if phase == 0:
            neighbour = [(get(f"o{at}"), offsets[part]) for at in range(2)]
            windows, choice = [both("u"), both("z"), neighbour, both("x")], (1, 2, 3)
        else:
            windows = [both(letter) for letter in "uzwxv"]
            choice = (1, 3, 4)
        before = phase * halves + part - 1
        whole = get(f"g{before // halves}{before % halves}")[0] if before >= 0 else None
        filled = []
        sizes = (group_cycles, cycle_dev, offsets[part], parts[part])
        return grams(
            place, tied(counts, name), get(f"u{own_units}"), whole, windows, choice, sizes, phase, frame_count, filled
        )

    def spot(phase, part):
        return get(f"s{phase}{part}"), (group_cycles, offsets[part], phase * (LAG // 2))

    for step, *names in ORDER:
        if step == "pause":
            token = pause(token, *names)
            continue
        for name in filter(known, names):
            value = get(name)
            if step == "wait":
                if name[0] == "g":
                    theirs, token = lax.optimization_barrier((value[1], token))
                    done[name] = [value[0], theirs]
                elif isinstance(value, (list, tuple)):
                    head, token = lax.optimization_barrier((value[0], token))
                    done[name] = [head, *value[1:]]
                else:
                    done[name], token = lax.optimization_barrier((value, token))
    whole = get(f"g1{halves - 1}")[0]
    spots = [spot(phase, part) for phase in range(2) for part in range(halves)]
    whole = fill(place, token, whole, spots[:-1])
    return fill(place, token, whole, spots[-1:])


def solution(mesh):
    placed = (P("frame", "mod"), P("mod"), P("mod"))
    return jax.shard_map(
        shards, mesh=mesh, in_specs=placed, out_specs=P("mod", "frame", None), check_vma=False
    )
```
